256 devices in a mesh: batch: 64 (over z, y, x_lo), tower: 4 (over x_hi, core).
Axes of the slice: x: 4 (x_hi: 2, x_lo: 2; x = x_hi * 2 + x_lo), y: 4, z: 8, core: 2. Of those that a mesh axis runs over, the one named last changes fastest.
Arguments:
- prompt_feats: bfloat16 [24576, 1152], P('batch', 'tower'), may hold values from -6 to 6
- response_feats: bfloat16 [24576, 1152], P('batch', 'tower'), may hold values from -6 to 6
- prompt_proj: bfloat16 [1152, 1152], P('tower'), may hold values from -0.1875 to 0.1875
- response_proj: bfloat16 [1152, 1152], P('tower'), may hold values from -0.1875 to 0.1875
- logit_scale: float32 [1], replicated, may hold values from 4 to 10
- logit_bias: float32 [1], replicated, may hold values from -2 to 0
- teacher: int32 [24576, 3072], P('batch'), may hold values from -127 to 127
- valid: int32 [24576, 8], P('batch'), may hold values from 0 to 1, as said below
Outputs:
- grad_prompt: bfloat16 [24576, 1152], P('batch', 'tower')
- grad_response: bfloat16 [24576, 1152], P('batch', 'tower')
- loss: float32 [1], replicated
The draws below stay inside these ranges and needn't reach their ends.
Inputs may be any that keep to these rules, and one draw needn't show every extreme that they name: valid holds only 0 and 1.
All inputs are finite; a program needn't handle non-finite values.
Results may differ from the reference program's by a relative error of at most 0.0065.
Values may be sent and summed in bfloat16 or wider, within the bound.
A program may use at most 128 MiB of HBM per device.

```python
import jax
import jax.numpy as jnp
from jax import lax

HID = 1152
E = 1152
TOK_DEV = 384
STEPS = 8
TOKENS = 24576
PAIRS = 3072


def draw_valid(key, part):
    key = jax.random.fold_in(key, 7)
    blocks = TOKENS // TOK_DEV
    block = jnp.arange(TOKENS, dtype=jnp.int32) // TOK_DEV
    level = 200 + 800 * block // (blocks - 1)
    roll = jax.random.randint(key, (TOKENS, STEPS), 0, 1000, dtype=jnp.int32)
    return (roll < level[:, None]).astype(jnp.int32)


def plant(result, stream_key, least, largest):
    longest = result.shape.index(max(result.shape))
    spots = []
    for shift in (0, 1):
        where = [jax.random.randint(jax.random.fold_in(stream_key, axis), (), 0, length) for axis, length in enumerate(result.shape)]
        where[longest] = (where[longest] + shift) % result.shape[longest]
        spots.append(tuple(where))
    return result.at[spots[0]].set(least).at[spots[1]].set(largest)


def steps_of(stream_key, dims, pieces, least, largest):
    factor_of = 1.0
    for axis_at, parts in pieces:
        steps = jax.random.uniform(jax.random.fold_in(jax.random.fold_in(stream_key, 6), axis_at), (parts,), jnp.float32, least / len(pieces), largest / len(pieces))
        factor_of = factor_of * jnp.repeat(jnp.exp(steps), dims[axis_at] // parts).reshape((-1,) + (1,) * (len(dims) - 1 - axis_at))
    return factor_of


def gaussian(own_key, extent, scale, limit, pieces=(), kind=jnp.bfloat16):
    entries = scale * jax.random.normal(own_key, extent, jnp.float32)
    if pieces:
        entries = entries * steps_of(own_key, extent, pieces, -0.22, 0.18)
    return jnp.clip(entries, -limit, limit).astype(kind)


def setup_inputs(seed: int = 0) -> dict:
    seeds = jax.random.split(jax.random.key(seed), 9)
    prompt_feats = gaussian(seeds[0], (TOKENS, HID), 1.0, 6.0, ((0, 64), (1, 4)))
    response_feats = gaussian(seeds[1], (TOKENS, HID), 1.0, 6.0, ((0, 64), (1, 4)))
    prompt_proj = gaussian(seeds[2], (HID, E), HID ** -0.5, 0.1875, ((0, 4),))
    response_proj = gaussian(seeds[3], (HID, E), HID ** -0.5, 0.1875, ((0, 4),))
    logit_scale = jnp.clip(jax.random.uniform(seeds[4], (1,), jnp.float32, 4.0, 10.0), 4.0, 10.0)
    logit_bias = jnp.clip(jax.random.uniform(seeds[5], (1,), jnp.float32, -2.0, 0.0), -2.0, 0.0)
    teacher = plant(jax.random.randint(seeds[6], (TOKENS, PAIRS), -127, 128), jax.random.fold_in(seeds[6], 1), -127, 127).astype(jnp.int32)
    valid = draw_valid(jax.random.fold_in(seeds[8], 71), 0)
    return dict(prompt_feats=prompt_feats, response_feats=response_feats, prompt_proj=prompt_proj, response_proj=response_proj, logit_scale=logit_scale, logit_bias=logit_bias, teacher=teacher, valid=valid)


def unit_rows(pre):
    norm = jnp.sqrt(lax.optimization_barrier(jnp.sum(pre * pre, axis=1, keepdims=True)) + 1e-06)
    return (pre / norm, norm)

def back_rows(grad, unit, norm):
    inner = lax.optimization_barrier(jnp.sum(unit * grad, axis=1, keepdims=True))
    return ((grad - unit * inner) / norm).astype(jnp.bfloat16)

def reference(prompt_feats, response_feats, prompt_proj, response_proj, logit_scale, logit_bias, teacher, valid):
    blocks = TOKENS // TOK_DEV
    pre_p = jnp.dot(prompt_feats, prompt_proj, preferred_element_type=jnp.float32)
    pre_r = jnp.dot(response_feats, response_proj, preferred_element_type=jnp.float32)
    unit_p, norm_p = unit_rows(pre_p)
    unit_r, norm_r = unit_rows(pre_r)
    emb_p = unit_p.astype(jnp.bfloat16)
    emb_r = unit_r.astype(jnp.bfloat16).reshape(blocks, TOK_DEV, E)
    scale = logit_scale[0]
    bias = logit_bias[0]

    def block_step(carry, inputs):
        grad_resp, loss_sum = carry
        prompt_blk, teach_blk, valid_blk, index = inputs
        grad_prompt_blk = jnp.zeros((TOK_DEV, E), jnp.float32)
        for step in range(STEPS):
            owner = jnp.mod(index - step, blocks).astype(jnp.int32)
            resp_blk = emb_r[owner]
            score = scale * lax.dot_general(prompt_blk, resp_blk, (((1,), (1,)), ((), ())), preferred_element_type=jnp.float32) + bias
            target = jax.nn.sigmoid(teach_blk[:, step * TOK_DEV:(step + 1) * TOK_DEV].astype(jnp.float32) / 32.0)
            weight = valid_blk[:, step:step + 1].astype(jnp.float32)
            loss_sum = loss_sum + jnp.sum(weight * (jax.nn.softplus(score) - target * score))
            coef = (scale * weight * (jax.nn.sigmoid(score) - target)).astype(jnp.bfloat16)
            grad_prompt_blk = grad_prompt_blk + jnp.dot(coef, resp_blk, preferred_element_type=jnp.float32)
            term = lax.dot_general(coef, prompt_blk, (((0,), (0,)), ((), ())), preferred_element_type=jnp.float32)
            grad_resp = grad_resp.at[owner].add(term)
        return ((grad_resp, loss_sum), grad_prompt_blk)
    start = (jnp.zeros((blocks, TOK_DEV, E), jnp.float32), jnp.zeros((), jnp.float32))
    inputs = (emb_p.reshape(blocks, TOK_DEV, E), teacher.reshape(blocks, TOK_DEV, PAIRS), valid.reshape(blocks, TOK_DEV, STEPS), jnp.arange(blocks, dtype=jnp.int32))
    (grad_resp, loss_sum), grad_prom = lax.scan(block_step, start, inputs)
    d_p = back_rows(grad_prom.reshape(TOKENS, E), unit_p, norm_p)
    d_r = back_rows(grad_resp.reshape(TOKENS, E), unit_r, norm_r)
    grad_prompt = lax.dot_general(d_p, prompt_proj, (((1,), (1,)), ((), ())), preferred_element_type=jnp.float32).astype(jnp.bfloat16)
    grad_response = lax.dot_general(d_r, response_proj, (((1,), (1,)), ((), ())), preferred_element_type=jnp.float32).astype(jnp.bfloat16)
    loss = (loss_sum / (TOKENS * PAIRS)).reshape(1)
    return (grad_prompt, grad_response, loss)
```

```python
import jax
import jax.numpy as jnp
from jax import lax
from jax.experimental import pallas as pl
from jax.experimental.pallas import tpu as pltpu
from jax.sharding import PartitionSpec as P

BF, F32 = jnp.bfloat16, jnp.float32
ROWS, FEAT, EMB, STEPS, BLOCKS, TOWER = 384, 288, 1152, 8, 64, 4
HALF, QUART = ROWS // 2, ROWS // 4
SLOTS = 5
NT = (((1,), (1,)), ((), ()))
TN = (((0,), (0,)), ((), ()))


def dot(a, b, dims=(((1,), (0,)), ((), ()))):
    return lax.dot_general(a, b, dims, preferred_element_type=F32)


def sigmoid(x):
    e = jnp.exp(-jnp.abs(x))
    return jnp.where(x >= 0, 1.0, e) / (1.0 + e)


def kernel(
    feats_r, feats_p, proj_r, proj_p, scale_ref, bias_ref, teach, valid,
    out_r, out_p, loss_ref,
    projs, feat_f, feat_n, fsend, frecv, unit, norm, emb_p, emb_r,
    traw, tsend, trecv, target, vown, vother, gp, gr, gpsend, gprecv,
    grsib_s, grsib_r, grsend, grrecv, dsend, dbuf, osend, oval,
    lmsg, lbuf, send_sem, recv_sem, loc_sem,
):
    b = lax.axis_index("batch")
    t = lax.axis_index("tower")
    l = lax.rem(b, 2)
    h, c = t // 2, lax.rem(t, 2)
    nb = b + 1 - 2 * l
    st = t + 1 - 2 * c
    ft = lax.rem(t + 2, TOWER)

    def dev(batch, tower):
        return {"batch": batch, "tower": tower}

    SIB, NEAR, NEARX, FAR = dev(b, st), dev(nb, t), dev(nb, st), dev(nb, ft)

    def ahead(i):
        return dev(lax.rem(b + 2 * i, BLOCKS), t)

    def behind(i):
        return dev(lax.rem(b + BLOCKS - 2 * i, BLOCKS), t)

    plane = (b // 8) * 8
    inplane = b - plane
    group_id = l * TOWER + t

    def group_peer(k):
        g = lax.rem(group_id + k, 8)
        return dev(b - l + g // TOWER, lax.rem(g, TOWER))

    def y_peer(k):
        return dev(plane + lax.rem(inplane + 2 * k, 8), t)

    def z_peer(k):
        return dev(lax.rem(b + 8 * k, BLOCKS), t)

    barrier = pltpu.get_barrier_semaphore()
    peers = [group_peer(k) for k in range(1, 8)]
    peers += [ahead(i) for i in range(1, SLOTS)] + [behind(i) for i in range(1, SLOTS)]
    peers += [y_peer(k) for k in range(1, 4)] + [z_peer(k) for k in range(2, 7)]
    for peer in peers:
        pl.semaphore_signal(barrier, inc=1, device_id=peer, device_id_type=pl.DeviceIdType.MESH)

    def quarter(half, core):
        return pl.ds(pl.multiple_of(half * HALF + core * QUART, 32), QUART)

    def part(core):
        return pl.ds(pl.multiple_of(core * QUART, 32), QUART)

    feats, proj = (feats_r, feats_p), (proj_r, proj_p)
    count = [0]
    local = []

    def load(src, dst):
        copy = pltpu.make_async_copy(src, dst, loc_sem.at[len(local)])
        copy.start()
        local.append(copy)
        return copy

    sends = []

    def remote(src, dst, to, start=True):
        k = count[0]
        count[0] += 1
        copy = pltpu.make_async_remote_copy(
            src_ref=src, dst_ref=dst, send_sem=send_sem.at[k], recv_sem=recv_sem.at[k],
            device_id=to, device_id_type=pl.DeviceIdType.MESH,
        )
        if start:
            copy.start()
            sends.append(copy)
        return copy

    own_proj, own_feat = [], []
    for w in (0, 1):
        own_proj.append(load(proj[w], projs.at[w, 0]))
        own_feat.append(load(feats[w].at[quarter(1 - h, c)], feat_f.at[w, 0]))
    own_teach = [load(teach.at[quarter(hh, c)], traw.at[hh]) for hh in (0, 1)]
    own_valid = [load(valid.at[quarter(hh, c)], vown.at[hh]) for hh in (0, 1)]

    pl.semaphore_wait(barrier, len(peers))

    to_sib, feat_sib, feat_near, feat_nearx = [], [], [], []
    for w in (0, 1):
        feat_sib.append(remote(feats[w].at[quarter(1 - h, 1 - c)], feat_f.at[w, 1], SIB))
        to_sib.append(remote(proj[w], projs.at[w, 1], SIB))
        feat_near.append(remote(feats[w].at[quarter(h, c)], feat_n.at[w, 0], NEAR))
        feat_nearx.append(remote(feats[w].at[quarter(h, 1 - c)], feat_n.at[w, 1], NEARX))
    valid_near = [remote(valid.at[quarter(hh, c)], vother.at[hh], NEAR) for hh in (0, 1)]

    partial = []
    for w in (0, 1):
        own_proj[w].wait()
        own_feat[w].wait()
        acc = dot(feat_f[w, 0], projs[w, 0])
        feat_sib[w].wait_recv()
        to_sib[w].wait_recv()
        acc += dot(feat_f[w, 1], projs[w, 1])
        fsend[w] = acc.astype(BF)
        partial.append(remote(fsend.at[w], frecv.at[w], FAR))

    for copy in own_teach:
        copy.wait()

    def steps_of(hh, s):
        both = traw[hh, :, s * ROWS:(s + 1) * ROWS].astype(F32)
        return jnp.where(h == 0, both, pltpu.roll(both, HALF, 1))[:, :HALF]

    for hh in (0, 1):
        for q in range(4):
            tsend[q, hh * QUART:(hh + 1) * QUART] = steps_of(hh, 2 * q).astype(BF)
    teach_near = remote(tsend, trecv, NEAR)

    def finish(w):
        feat_near[w].wait_recv()
        feat_nearx[w].wait_recv()
        pre = dot(feat_n[w, 0], projs[w, 0]) + dot(feat_n[w, 1], projs[w, 1])
        partial[w].wait_recv()
        pre = pre + frecv[w].astype(F32)
        length = jnp.sqrt(jnp.sum(pre * pre, axis=1, keepdims=True) + 1e-06)
        norm[w] = jnp.broadcast_to(length, (QUART, 128))
        u = pre / length
        unit[w] = u
        return u.astype(BF)

    emb_r[0, part(c)] = finish(0)
    band = [None] * SLOTS
    for i in (3, 2, 1):
        band[i] = remote(emb_r.at[0, part(c)], emb_r.at[i, part(c)], ahead(i))
    band[4] = remote(emb_r.at[0, part(c)], emb_r.at[4, part(c)], ahead(4), start=False)

    @pl.when(l == 0)
    def _():
        band[4].start()

    resp_sib = [None] * SLOTS
    resp_sib[0] = remote(emb_r.at[0, part(c)], emb_r.at[0, part(c)], SIB)

    emb_p[0, part(h)] = finish(1)
    p_far = remote(emb_p.at[0, part(h)], emb_p.at[1, part(h)], FAR)
    p_near = remote(emb_p.at[0, part(h)], emb_p.at[1, part(h)], NEAR)

    for hh in (0, 1):
        for q in range(4):
            target[1, q, hh * QUART:(hh + 1) * QUART] = sigmoid(steps_of(hh, 2 * q + 1) / 32.0)

    p_far.wait_recv()
    p_opp = remote(emb_p.at[1, part(1 - h)], emb_p.at[0, part(1 - h)], NEAR)

    teach_near.wait_recv()
    for q in range(4):
        target[0, q] = sigmoid(trecv[q].astype(F32) / 32.0)

    for i in (1, 2, 3):
        band[i].wait_recv()
        resp_sib[i] = remote(emb_r.at[i, part(c)], emb_r.at[i, part(c)], SIB)
    resp_sib[4] = remote(emb_r.at[4, part(c)], emb_r.at[4, part(c)], SIB, start=False)

    @pl.when(l == 0)
    def _():
        band[4].wait_recv()
        resp_sib[4].start()

    for hh in (0, 1):
        own_valid[hh].wait()
        valid_near[hh].wait_recv()
    p_near.wait_recv()
    p_opp.wait_recv()
    for i in (3, 2, 1, 0):
        resp_sib[i].wait_recv()

    @pl.when(l == 0)
    def _():
        resp_sib[4].wait_recv()

    scale, bias = scale_ref[0], bias_ref[0]
    loss = jnp.zeros((8, HALF), F32)
    gr_sib, gr_home = [None] * SLOTS, [None] * SLOTS

    def push(i, slot):
        grsib_s[i] = gr[slot, part(1 - c)].astype(BF)

    for q in (3, 2, 1, 0):
        for kind in (0, 1):
            slot = q if kind == 0 else q + 1 - l
            weight = (vother if kind == 0 else vown)[:, :, 2 * q + kind:2 * q + kind + 1]
            weight = weight.reshape(HALF, 1).astype(F32)
            goal = target[kind, q]
            z = scale * dot(emb_p[kind], emb_r[slot], NT) + bias
            e = jnp.exp(-jnp.abs(z))
            soft = jnp.maximum(z, 0.0) + jnp.log1p(e)
            sig = jnp.where(z >= 0, 1.0, e) / (1.0 + e)
            cost = weight * (soft - goal * z)
            loss = loss + jnp.sum(cost.reshape(HALF // 8, 8, HALF), axis=0)
            coef = (scale * weight * (sig - goal)).astype(BF)
            term_p = dot(coef, emb_r[slot])
            term_r = dot(coef, emb_p[kind], TN)
            if q == 3:
                gp[kind] = term_p
            else:
                gp[kind] += term_p
            if kind == 0:
                gr[q] = term_r
            elif q == 3:
                @pl.when(l == 0)
                def _():
                    gr[4] = term_r

                @pl.when(l == 1)
                def _():
                    gr[3] += term_r
            else:
                gr[slot] += term_r

    gpsend[0] = gp[0, part(1 - h)].astype(BF)
    g_opp = remote(gpsend.at[0], gprecv.at[0], NEAR)
    for i in (3, 2, 1, 0):
        push(i, i)
        gr_sib[i] = remote(grsib_s.at[i], grsib_r.at[i], SIB)
    gr_sib[4] = remote(grsib_s.at[4], grsib_r.at[4], SIB, start=False)

    @pl.when(l == 0)
    def _():
        push(4, 4)
        gr_sib[4].start()

    gpsend[1] = gp[1, part(h)].astype(BF)
    g_near = remote(gpsend.at[1], gprecv.at[1], NEAR)

    for i in (3, 2, 1):
        gr_sib[i].wait_recv()
        grsend[i] = (gr[i, part(c)] + grsib_r[i].astype(F32)).astype(BF)
        gr_home[i] = remote(grsend.at[i], grrecv.at[i], behind(i))
    gr_home[4] = remote(grsend.at[4], grrecv.at[4], behind(4), start=False)

    @pl.when(l == 0)
    def _():
        gr_sib[4].wait_recv()
        grsend[4] = (gr[4, part(c)] + grsib_r[4].astype(F32)).astype(BF)
        gr_home[4].start()

    g_opp.wait_recv()
    gpsend[2] = (gp[1, part(1 - h)] + gprecv[0].astype(F32)).astype(BF)
    g_far = remote(gpsend.at[2], gprecv.at[2], FAR)

    def gather(stage, value, me, total, peer_of):
        lmsg[stage] = jnp.full((8, 128), value, F32)
        lbuf[stage, me] = lmsg[stage]
        copies = [remote(lmsg.at[stage], lbuf.at[stage, me], peer_of(k)) for k in range(1, total)]
        for copy in copies:
            copy.wait_recv()
        return jnp.sum(lbuf[stage, :total]) / 1024.0

    total = gather(0, jnp.sum(loss), group_id, 8, group_peer)
    total = gather(1, total, inplane // 2, 4, y_peer)
    total = gather(2, total, b // 8, 8, z_peer)
    loss_ref[0] = total / (ROWS * BLOCKS * STEPS * ROWS)

    d_far, d_sib, o_near, o_nearx = [None] * 2, [None] * 2, [None] * 2, [None] * 2

    def back(w, g):
        u = unit[w]
        inner = jnp.sum(u * g, axis=1, keepdims=True)
        d = ((g - u * inner) / norm[w, :, 0:1]).astype(BF)
        dsend[w] = d
        d_far[w] = remote(dsend.at[w], dbuf.at[w, part(c)], FAR)
        osend[w, 0] = dot(d, projs[w, 0], NT).astype(BF)
        osend[w, 1] = dot(d, projs[w, 1], NT).astype(BF)
        o_near[w] = remote(osend.at[w, 0], oval.at[w, h, part(c)], NEAR)
        o_nearx[w] = remote(osend.at[w, 1], oval.at[w, h, part(c)], NEARX)

    g_near.wait_recv()
    g_far.wait_recv()
    back(1, gp[0, part(h)] + gprecv[1].astype(F32) + gprecv[2].astype(F32))

    gr_sib[0].wait_recv()
    gr[0, part(c)] += grsib_r[0].astype(F32)
    for i in (1, 2, 3):
        gr_home[i].wait_recv()
        gr[0, part(c)] += grrecv[i].astype(F32)

    @pl.when(l == 0)
    def _():
        gr_home[4].wait_recv()
        gr[0, part(c)] += grrecv[4].astype(F32)

    back(0, gr[0, part(c)])

    outs = (out_r, out_p)
    for w in (1, 0):
        d_far[w].wait_recv()
        d_sib[w] = remote(dbuf.at[w, part(c)], dbuf.at[w, part(c)], SIB)
    for w in (1, 0):
        d_sib[w].wait_recv()
        oval[w, 1 - h] = dot(dbuf[w], projs[w, 0], NT).astype(BF)
        o_near[w].wait_recv()
        o_nearx[w].wait_recv()
        for hh in (0, 1):
            load(oval.at[w, hh], outs[w].at[hh * HALF:(hh + 1) * HALF])
    for copy in local[-4:]:
        copy.wait()
    for copy in sends:
        copy.wait_send()

    @pl.when(l == 0)
    def _():
        for copy in (band[4], resp_sib[4], gr_sib[4], gr_home[4]):
            copy.wait_send()


def on_device(
    prompt_feats, response_feats, prompt_proj, response_proj,
    logit_scale, logit_bias, teacher, valid,
):
    anywhere = pl.BlockSpec(memory_space=pl.ANY)
    scalar = pl.BlockSpec(memory_space=pltpu.SMEM)

    def vm(*shape, kind=BF):
        return pltpu.VMEM(shape, kind)

    grad_response, grad_prompt, loss = pl.pallas_call(
        kernel,
        out_shape=(
            jax.ShapeDtypeStruct((ROWS, FEAT), BF),
            jax.ShapeDtypeStruct((ROWS, FEAT), BF),
            jax.ShapeDtypeStruct((1,), F32),
        ),
        in_specs=[anywhere] * 4 + [scalar] * 2 + [anywhere] * 2,
        out_specs=(anywhere, anywhere, scalar),
        scratch_shapes=[
            vm(2, 2, FEAT, EMB),
            vm(2, 2, QUART, FEAT),
            vm(2, 2, QUART, FEAT),
            vm(2, QUART, EMB),
            vm(2, QUART, EMB),
            vm(2, QUART, EMB, kind=F32),
            vm(2, QUART, 128, kind=F32),
            vm(2, HALF, EMB),
            vm(SLOTS, HALF, EMB),
            vm(2, QUART, STEPS * ROWS, kind=jnp.int32),
            vm(4, HALF, HALF),
            vm(4, HALF, HALF),
            vm(2, 4, HALF, HALF, kind=F32),
            vm(2, QUART, STEPS, kind=jnp.int32),
            vm(2, QUART, STEPS, kind=jnp.int32),
            vm(2, HALF, EMB, kind=F32),
            vm(SLOTS, HALF, EMB, kind=F32),
            vm(3, QUART, EMB),
            vm(3, QUART, EMB),
            vm(SLOTS, QUART, EMB),
            vm(SLOTS, QUART, EMB),
            vm(SLOTS, QUART, EMB),
            vm(SLOTS, QUART, EMB),
            vm(2, QUART, EMB),
            vm(2, HALF, EMB),
            vm(2, 2, QUART, FEAT),
            vm(2, 2, HALF, FEAT),
            vm(3, 8, 128, kind=F32),
            vm(3, 8, 8, 128, kind=F32),
            pltpu.SemaphoreType.DMA((64,)),
            pltpu.SemaphoreType.DMA((64,)),
            pltpu.SemaphoreType.DMA((16,)),
        ],
        compiler_params=pltpu.CompilerParams(
            collective_id=0, has_side_effects=True, vmem_limit_bytes=56 * 2**20
        ),
        name="band",
    )(
        response_feats, prompt_feats, response_proj, prompt_proj,
        logit_scale, logit_bias, teacher, valid,
    )
    return grad_prompt, grad_response, loss


def solution(mesh):
    in_specs = (
        P("batch", "tower"), P("batch", "tower"), P("tower", None), P("tower", None),
        P(), P(), P("batch", None), P("batch", None),
    )
    out_specs = (P("batch", "tower"), P("batch", "tower"), P())
    return jax.shard_map(
        on_device, mesh=mesh, in_specs=in_specs, out_specs=out_specs, check_vma=False
    )
```

```python
import jax
import jax.numpy as jnp
from jax import lax
from jax.experimental import pallas as pl
from jax.experimental.pallas import tpu as pltpu
from jax.sharding import PartitionSpec as P

BF, F32 = jnp.bfloat16, jnp.float32
ROWS, FEAT, EMB, STEPS, BLOCKS, TOWER = 384, 288, 1152, 8, 64, 4
HALF, QUART = ROWS // 2, ROWS // 4
SLOTS, PIECE = 5, 48
NT = (((1,), (1,)), ((), ()))
TN = (((0,), (0,)), ((), ()))


def dot(a, b, dims=(((1,), (0,)), ((), ()))):
    return lax.dot_general(a, b, dims, preferred_element_type=F32)


def sigmoid(x):
    e = jnp.exp(-jnp.abs(x))
    return jnp.where(x >= 0, 1.0, e) / (1.0 + e)


def kernel(
    feats_r, feats_p, proj_r, proj_p, scale_ref, bias_ref, teach, valid,
    out_r, out_p, loss_ref,
    fcols, frows, projs, feat_f, feat_n, fsend, frecv, unit, norm, emb_p, emb_r,
    traw, tsend, trecv, target, vcols, vrows, gp, gr, gpsend, gprecv,
    grsib_s, grsib_r, grsend, grrecv, dsend, dbuf, osend, onear, oval,
    lmsg, lbuf, send_sem, recv_sem, loc_sem,
):
    b = lax.axis_index("batch")
    t = lax.axis_index("tower")
    l = lax.rem(b, 2)
    h, c = t // 2, lax.rem(t, 2)
    nb = b + 1 - 2 * l
    st = t + 1 - 2 * c
    ft = lax.rem(t + 2, TOWER)
    plane = (b // 8) * 8
    inplane = b - plane
    y = inplane // 2
    odd = lax.rem(y, 2)

    def dev(batch, tower):
        return {"batch": batch, "tower": tower}

    SIB, NEAR, NEARX, FAR = dev(b, st), dev(nb, t), dev(nb, st), dev(nb, ft)
    UP, DOWN = dev(plane + lax.rem(inplane + 2, 8), t), dev(plane + lax.rem(inplane + 6, 8), t)
    PAIR = dev(b + 2 - 4 * odd, t)
    AHEAD, BEHIND = dev(lax.rem(b + 8, BLOCKS), t), dev(lax.rem(b + BLOCKS - 8, BLOCKS), t)
    group_id = l * TOWER + t

    def group_peer(k):
        g = lax.rem(group_id + k, 8)
        return dev(b - l + g // TOWER, lax.rem(g, TOWER))

    def y_peer(k):
        return dev(plane + lax.rem(inplane + 2 * k, 8), t)

    def z_peer(k):
        return dev(lax.rem(b + 8 * k, BLOCKS), t)

    barrier = pltpu.get_barrier_semaphore()
    peers = [group_peer(k) for k in range(1, 8)]
    peers += [y_peer(k) for k in range(1, 4)] + [z_peer(k) for k in range(1, 8)]
    for peer in peers:
        pl.semaphore_signal(barrier, inc=1, device_id=peer, device_id_type=pl.DeviceIdType.MESH)

    def rows_at(start, count):
        return pl.ds(pl.multiple_of(start, 16), count)

    def quarter(half, core):
        return rows_at(half * HALF + core * QUART, QUART)

    def part(core):
        return rows_at(core * QUART, QUART)

    def piece(slot, core, k):
        return rows_at(slot * HALF + core * QUART + k * PIECE, PIECE)

    def cut(k):
        return slice(k * PIECE, (k + 1) * PIECE)

    feats, proj = (feats_r, feats_p), (proj_r, proj_p)
    local = []

    def load(src, dst):
        copy = pltpu.make_async_copy(src, dst, loc_sem.at[len(local)])
        copy.start()
        local.append(copy)
        return copy

    links = []

    class Link:
        def __init__(self, copy):
            self.copy, self.waited = copy, False

        def start(self):
            self.copy.start()

        def wait_recv(self):
            self.waited = True
            self.copy.wait_recv()

    def remote(src, dst, to, start=True):
        k = len(links)
        link = Link(
            pltpu.make_async_remote_copy(
                src_ref=src, dst_ref=dst, send_sem=send_sem.at[k], recv_sem=recv_sem.at[k],
                device_id=to, device_id_type=pl.DeviceIdType.MESH,
            )
        )
        if start:
            link.start()
        links.append(link)
        return link

    def close():
        for link in links:
            if not link.waited:
                link.copy.wait_recv()
            link.copy.wait_send()

    own_feat = [load(feats[w], fcols.at[w]) for w in (0, 1)]
    own_proj = [load(proj[w], projs.at[w, 0]) for w in (0, 1)]
    own_teach = [load(teach.at[quarter(hh, c)], traw.at[hh]) for hh in (0, 1)]
    own_valid = load(valid, vcols.at[1])

    for w in (0, 1):
        own_feat[w].wait()
        frows[w] = fcols[w].astype(F32).T.astype(BF)
    pl.semaphore_wait(barrier, len(peers))

    to_sib, feat_sib, feat_near, feat_nearx = [], [], [], []

    def enter(w):
        feat_sib.append(remote(frows.at[w, quarter(1 - h, 1 - c)], feat_f.at[w], SIB))
        to_sib.append(remote(proj[w], projs.at[w, 1], SIB))
        feat_near.append(remote(frows.at[w, quarter(h, c)], feat_n.at[w, 0], NEAR))
        feat_nearx.append(remote(frows.at[w, quarter(h, 1 - c)], feat_n.at[w, 1], NEARX))

    partial = []

    def half_sum(w):
        own_proj[w].wait()
        acc = dot(frows[w, quarter(1 - h, c)], projs[w, 0])
        feat_sib[w].wait_recv()
        to_sib[w].wait_recv()
        acc += dot(feat_f[w], projs[w, 1])
        fsend[w] = acc.astype(BF)
        partial.append(remote(fsend.at[w], frecv.at[w], FAR))

    enter(0)
    own_proj[0].wait()
    first = dot(frows[0, quarter(1 - h, c)], projs[0, 0])
    feat_sib[0].wait_recv()
    to_sib[0].wait_recv()
    enter(1)
    fsend[0] = (first + dot(feat_f[0], projs[0, 1])).astype(BF)
    partial.append(remote(fsend.at[0], frecv.at[0], FAR))
    half_sum(1)

    for copy in own_teach:
        copy.wait()
    early = lax.broadcasted_iota(jnp.int32, (1, ROWS), 1) < HALF

    def steps_of(hh, s):
        a = traw[hh, :, s * ROWS:(s + 1) * ROWS].astype(F32)
        d = traw[hh, :, (s + 2) * ROWS:(s + 3) * ROWS].astype(F32)
        keep = jnp.where(h == 0, a, d)
        turn = pltpu.roll(jnp.where(h == 0, d, a), HALF, 1)
        lanes = lax.broadcasted_iota(jnp.int32, (QUART, ROWS), 1)
        return jnp.where((lanes < HALF) == (h == 0), keep, turn)

    for p in (0, 1):
        for hh in (0, 1):
            tsend[p, hh * QUART:(hh + 1) * QUART] = steps_of(hh, 4 * p).astype(BF)
    teach_near = remote(tsend, trecv, NEAR)
    valid_near = remote(valid, vcols.at[0], NEAR)
    for p in (0, 1):
        for hh in (0, 1):
            target[1, p, hh * QUART:(hh + 1) * QUART] = sigmoid(steps_of(hh, 4 * p + 1) / 32.0)
    gr[4 * HALF:] = jnp.zeros((HALF, EMB), F32)

    def finish(w):
        feat_near[w].wait_recv()
        feat_nearx[w].wait_recv()
        pre = dot(feat_n[w, 0], projs[w, 0]) + dot(feat_n[w, 1], projs[w, 1])
        partial[w].wait_recv()
        pre = pre + frecv[w].astype(F32)
        length = jnp.sqrt(jnp.sum(pre * pre, axis=1, keepdims=True) + 1e-06)
        norm[w] = jnp.broadcast_to(length, (QUART, 128))
        u = pre / length
        unit[w] = u
        return u.astype(BF)

    pieces = range(ROWS // 4 // PIECE)
    up_from, down_from, pair_from = (y // 3) * 4, ((y + 3) // 4) * 4, 1 + 2 * odd

    def relay(src, dst, to, start=True):
        return [
            remote(emb_r.at[piece(src, c, k)], emb_r.at[piece(dst, c, k)], to, start)
            for k in pieces
        ]

    def resp_over(slot):
        at = quarter(slot, c)
        return remote(emb_r.at[at], emb_r.at[at], SIB)

    emb_r[part(c)] = finish(0)
    zhop = relay(0, 4, AHEAD)
    up, down = relay(up_from, 1, UP, False), relay(down_from, 3, DOWN, False)
    pair = relay(pair_from, 2, PAIR, False)

    @pl.when(y < 3)
    def _():
        for link in up:
            link.start()

    @pl.when(y == 0)
    def _():
        for link in down:
            link.start()

    resp_sib = [None] * SLOTS
    resp_sib[0] = resp_over(0)

    fresh = finish(1)
    emb_p[0, part(h)] = fresh
    p_far, p_near, p_opp = [], [], []
    for k in pieces:
        at = rows_at(h * QUART + k * PIECE, PIECE)
        p_far.append(remote(emb_p.at[0, at], emb_p.at[1, at], FAR))
        p_near.append(remote(emb_p.at[0, at], emb_p.at[1, at], NEAR))

    for k in pieces:
        zhop[k].wait_recv()

        @pl.when(y == 3)
        def _():
            up[k].start()

        @pl.when(y > 0)
        def _():
            down[k].start()

    resp_sib[4] = resp_over(4)

    teach_near.wait_recv()
    for p in (0, 1):
        target[0, p] = sigmoid(trecv[p].astype(F32) / 32.0)
    own_valid.wait()
    valid_near.wait_recv()
    for kind in (0, 1):
        vrows[kind] = vcols[kind].astype(F32).T

    for k in pieces:
        @pl.when(odd == 0)
        def _():
            up[k].wait_recv()

        @pl.when(odd == 1)
        def _():
            down[k].wait_recv()

        pair[k].start()
        p_far[k].wait_recv()
        at = rows_at((1 - h) * QUART + k * PIECE, PIECE)
        p_opp.append(remote(emb_p.at[1, at], emb_p.at[0, at], NEAR))

    for k in pieces:
        @pl.when(odd == 1)
        def _():
            up[k].wait_recv()

        @pl.when(odd == 0)
        def _():
            down[k].wait_recv()

    resp_sib[3], resp_sib[1] = resp_over(3), resp_over(1)
    for k in pieces:
        pair[k].wait_recv()
    resp_sib[2] = resp_over(2)
    for k in pieces:
        p_near[k].wait_recv()
        p_opp[k].wait_recv()
    for i in (4, 3, 2, 1, 0):
        resp_sib[i].wait_recv()

    scale, bias = scale_ref[0], bias_ref[0]
    loss = jnp.zeros((8, ROWS), F32)
    for p in (1, 0):
        for kind in (0, 1):
            slots = pl.ds(pl.multiple_of((2 * p + kind * (1 - l)) * HALF, 64), ROWS)
            step = 4 * p + kind
            weight = jnp.concatenate(
                [
                    jnp.where(
                        early,
                        vrows[kind, quarter(hh, c), step:step + 1],
                        vrows[kind, quarter(hh, c), step + 2:step + 3],
                    )
                    for hh in (0, 1)
                ],
                axis=0,
            )
            goal = target[kind, p]
            z = scale * dot(emb_p[kind], emb_r[slots], NT) + bias
            e = jnp.exp(-jnp.abs(z))
            soft = jnp.maximum(z, 0.0) + jnp.log1p(e)
            sig = jnp.where(z >= 0, 1.0, e) / (1.0 + e)
            cost = weight * (soft - goal * z)
            loss = loss + jnp.sum(cost.reshape(HALF // 8, 8, ROWS), axis=0)
            coef = (scale * weight * (sig - goal)).astype(BF)
            term_p = dot(coef, emb_r[slots])
            term_r = dot(coef, emb_p[kind], TN)
            if p == 1:
                gp[kind] = term_p
            else:
                gp[kind] += term_p
            if kind == 0:
                gr[slots] = term_r
            else:
                gr[slots] += term_r

    gathers = []

    def gather(value, me, total, peer_of):
        stage = len(gathers)
        lmsg[stage] = jnp.full((8, 128), value, F32)
        lbuf[stage, me] = lmsg[stage]
        gathers.append(
            [remote(lmsg.at[stage], lbuf.at[stage, me], peer_of(k)) for k in range(1, total)]
        )

    def gathered(stage, total):
        for copy in gathers[stage]:
            copy.wait_recv()
        return jnp.sum(lbuf[stage, :total]) / 1024.0

    gr_sib = [None] * SLOTS

    def push(i):
        grsib_s[i] = gr[quarter(i, 1 - c)].astype(BF)
        gr_sib[i] = remote(grsib_s.at[i], grsib_r.at[i], SIB)

    g_opp, g_far = [], []
    push(2)
    gpsend[0] = gp[0, part(1 - h)].astype(BF)
    for k in pieces:
        g_opp.append(remote(gpsend.at[0, cut(k)], gprecv.at[0, cut(k)], NEAR))
    push(1)
    push(3)
    gpsend[1] = gp[1, part(h)].astype(BF)
    g_near = remote(gpsend.at[1], gprecv.at[1], NEAR)
    push(4)
    push(0)
    gather(jnp.sum(loss), group_id, 8, group_peer)

    def join(i):
        gr_sib[i].wait_recv()
        gr[quarter(i, c)] += grsib_r[i].astype(F32)

    def hop(i, slot, to, start=True):
        return [
            remote(grsend.at[i, cut(k)], grrecv.at[i, cut(k)], to, start) for k in pieces
        ]

    def fill(i, slot, k):
        grsend[i, cut(k)] = gr[piece(slot, c, k)].astype(BF)

    def add(slot, i, k):
        gr[piece(slot, c, k)] += grrecv[i, cut(k)].astype(F32)

    join(2)
    for k in pieces:
        fill(2, 2, k)
    home_pair = hop(2, 2, PAIR)
    join(1)
    join(3)
    home_down, home_up = hop(1, 1, DOWN, False), hop(3, 3, UP, False)

    @pl.when(odd == 0)
    def _():
        for k in pieces:
            fill(3, 3, k)
            home_up[k].start()

    @pl.when(odd == 1)
    def _():
        for k in pieces:
            fill(1, 1, k)
            home_down[k].start()

    join(4)
    join(0)
    for k in pieces:
        g_opp[k].wait_recv()
        at = rows_at((1 - h) * QUART + k * PIECE, PIECE)
        gpsend[2, cut(k)] = (gp[1, at] + gprecv[0, cut(k)].astype(F32)).astype(BF)
        g_far.append(remote(gpsend.at[2, cut(k)], gprecv.at[2, cut(k)], FAR))
        home_pair[k].wait_recv()
        add(pair_from, 2, k)

        @pl.when(odd == 0)
        def _():
            fill(1, 1, k)
            home_down[k].start()

        @pl.when(odd == 1)
        def _():
            fill(3, 3, k)
            home_up[k].start()

    gather(gathered(0, 8), y, 4, y_peer)
    home_z = hop(4, 4, BEHIND, False)
    for k in pieces:
        home_down[k].wait_recv()
        add(up_from, 1, k)
        home_up[k].wait_recv()
        add(down_from, 3, k)
        fill(4, 4, k)
        home_z[k].start()
    gather(gathered(1, 4), b // 8, 8, z_peer)

    d_far, d_sib, o_near, o_nearx = [None] * 2, [None] * 2, [None] * 2, [None] * 2

    def back(w, g):
        u = unit[w]
        inner = jnp.sum(u * g, axis=1, keepdims=True)
        d = ((g - u * inner) / norm[w, :, 0:1]).astype(BF)
        dsend[w] = d
        d_far[w] = remote(dsend.at[w], dbuf.at[w, part(c)], FAR)
        osend[w, 0] = dot(d, projs[w, 0], NT).astype(BF)
        osend[w, 1] = dot(d, projs[w, 1], NT).astype(BF)
        o_near[w] = remote(osend.at[w, 0], onear.at[w, part(c)], NEAR)
        o_nearx[w] = remote(osend.at[w, 1], onear.at[w, part(c)], NEARX)

    g_near.wait_recv()
    for link in g_far:
        link.wait_recv()
    back(1, gp[0, part(h)] + gprecv[1].astype(F32) + gprecv[2].astype(F32))

    for k in pieces:
        home_z[k].wait_recv()
        add(0, 4, k)
    back(0, gr[part(c)])
    loss_ref[0] = gathered(2, 8) / (ROWS * BLOCKS * STEPS * ROWS)

    outs = (out_r, out_p)

    def place(w, half, block):
        @pl.when(half == 0)
        def _():
            oval[w, :, :HALF] = block

        @pl.when(half == 1)
        def _():
            oval[w, :, HALF:] = block

    written = []
    d_far[1].wait_recv()
    d_sib[1] = remote(dbuf.at[1, part(c)], dbuf.at[1, part(c)], SIB)
    for w in (1, 0):
        o_near[w].wait_recv()
        o_nearx[w].wait_recv()
        place(w, h, onear[w].astype(F32).T.astype(BF))
        if w == 0:
            d_far[0].wait_recv()
            d_sib[0] = remote(dbuf.at[0, part(c)], dbuf.at[0, part(c)], SIB)
        d_sib[w].wait_recv()
        place(w, 1 - h, dot(projs[w, 0], dbuf[w], NT).astype(BF))
        written.append(load(oval.at[w], outs[w]))
    for copy in written:
        copy.wait()
    close()


def on_device(
    prompt_feats, response_feats, prompt_proj, response_proj,
    logit_scale, logit_bias, teacher, valid,
):
    anywhere = pl.BlockSpec(memory_space=pl.ANY)
    scalar = pl.BlockSpec(memory_space=pltpu.SMEM)

    def vm(*shape, kind=BF):
        return pltpu.VMEM(shape, kind)

    grad_response, grad_prompt, loss = pl.pallas_call(
        kernel,
        out_shape=(
            jax.ShapeDtypeStruct((FEAT, ROWS), BF),
            jax.ShapeDtypeStruct((FEAT, ROWS), BF),
            jax.ShapeDtypeStruct((1,), F32),
        ),
        in_specs=[anywhere] * 4 + [scalar] * 2 + [anywhere] * 2,
        out_specs=(anywhere, anywhere, scalar),
        scratch_shapes=[
            vm(2, FEAT, ROWS),
            vm(2, ROWS, FEAT),
            vm(2, 2, FEAT, EMB),
            vm(2, QUART, FEAT),
            vm(2, 2, QUART, FEAT),
            vm(2, QUART, EMB),
            vm(2, QUART, EMB),
            vm(2, QUART, EMB, kind=F32),
            vm(2, QUART, 128, kind=F32),
            vm(2, HALF, EMB),
            vm(SLOTS * HALF, EMB),
            vm(2, QUART, STEPS * ROWS, kind=jnp.int32),
            vm(2, HALF, ROWS),
            vm(2, HALF, ROWS),
            vm(2, 2, HALF, ROWS, kind=F32),
            vm(2, STEPS, ROWS, kind=jnp.int32),
            vm(2, ROWS, STEPS, kind=F32),
            vm(2, HALF, EMB, kind=F32),
            vm(SLOTS * HALF, EMB, kind=F32),
            vm(3, QUART, EMB),
            vm(3, QUART, EMB),
            vm(SLOTS, QUART, EMB),
            vm(SLOTS, QUART, EMB),
            vm(SLOTS, QUART, EMB),
            vm(SLOTS, QUART, EMB),
            vm(2, QUART, EMB),
            vm(2, HALF, EMB),
            vm(2, 2, QUART, FEAT),
            vm(2, HALF, FEAT),
            vm(2, FEAT, ROWS),
            vm(3, 8, 128, kind=F32),
            vm(3, 8, 8, 128, kind=F32),
            pltpu.SemaphoreType.DMA((104,)),
            pltpu.SemaphoreType.DMA((104,)),
            pltpu.SemaphoreType.DMA((16,)),
        ],
        compiler_params=pltpu.CompilerParams(
            collective_id=0, has_side_effects=True, vmem_limit_bytes=56 * 2**20
        ),
        name="band",
    )(
        response_feats.T, prompt_feats.T, response_proj, prompt_proj,
        logit_scale, logit_bias, teacher, valid.T,
    )
    return grad_prompt.T, grad_response.T, loss


def solution(mesh):
    in_specs = (
        P("batch", "tower"), P("batch", "tower"), P("tower", None), P("tower", None),
        P(), P(), P("batch", None), P("batch", None),
    )
    out_specs = (P("batch", "tower"), P("batch", "tower"), P())
    return jax.shard_map(
        on_device, mesh=mesh, in_specs=in_specs, out_specs=out_specs, check_vma=False
    )
```

```python
import jax
import jax.numpy as jnp
from jax import lax
from jax.experimental import pallas as pl
from jax.experimental.pallas import tpu as pltpu
from jax.sharding import PartitionSpec as P

BF, F32 = jnp.bfloat16, jnp.float32
ROWS, FEAT, EMB, STEPS, BLOCKS, TOWER = 384, 288, 1152, 8, 64, 4
HALF, QUART = ROWS // 2, ROWS // 4
SLOTS, PIECE = 5, 32
NT = (((1,), (1,)), ((), ()))
TN = (((0,), (0,)), ((), ()))


def dot(a, b, dims=(((1,), (0,)), ((), ()))):
    return lax.dot_general(a, b, dims, preferred_element_type=F32)


def sigmoid(x):
    e = jnp.exp(-jnp.abs(x))
    return jnp.where(x >= 0, 1.0, e) / (1.0 + e)


def kernel(
    feats_r, feats_p, proj_r, proj_p, scale_ref, bias_ref, teach, valid,
    out_r, out_p, loss_ref,
    fcols, frows, projs, part_sum, sib_send, sib_recv, feat_n, fsend, frecv, unit, norm, emb_p, emb_r,
    traw, tsend, trecv, target, vcols, vrows, coefs, gp, gr, gpsend, gprecv,
    grsib_s, grsib_r, grsend, grrecv, dsend, dbuf, osend, onear, oval,
    lmsg, lbuf, send_sem, recv_sem, loc_sem,
):
    b = lax.axis_index("batch")
    t = lax.axis_index("tower")
    l = lax.rem(b, 2)
    h, c = t // 2, lax.rem(t, 2)
    nb = b + 1 - 2 * l
    st = t + 1 - 2 * c
    ft = lax.rem(t + 2, TOWER)
    plane = (b // 8) * 8
    inplane = b - plane
    y = inplane // 2
    odd = lax.rem(y, 2)

    def dev(batch, tower):
        return {"batch": batch, "tower": tower}

    SIB, NEAR, NEARX, FAR = dev(b, st), dev(nb, t), dev(nb, st), dev(nb, ft)
    UP, DOWN = dev(plane + lax.rem(inplane + 2, 8), t), dev(plane + lax.rem(inplane + 6, 8), t)
    PAIR = dev(b + 2 - 4 * odd, t)
    AHEAD, BEHIND = dev(lax.rem(b + 8, BLOCKS), t), dev(lax.rem(b + BLOCKS - 8, BLOCKS), t)
    group_id = l * TOWER + t

    def group_peer(k):
        g = lax.rem(group_id + k, 8)
        return dev(b - l + g // TOWER, lax.rem(g, TOWER))

    def y_peer(k):
        return dev(plane + lax.rem(inplane + 2 * k, 8), t)

    def z_peer(k):
        return dev(lax.rem(b + 8 * k, BLOCKS), t)

    barrier = pltpu.get_barrier_semaphore()
    peers = [group_peer(k) for k in range(1, 8)]
    peers += [y_peer(k) for k in range(1, 4)] + [z_peer(k) for k in range(1, 8)]
    for peer in peers:
        pl.semaphore_signal(barrier, inc=1, device_id=peer, device_id_type=pl.DeviceIdType.MESH)

    def rows_at(start, count):
        return pl.ds(pl.multiple_of(start, 16), count)

    def quarter(half, core):
        return rows_at(half * HALF + core * QUART, QUART)

    def part(core):
        return rows_at(core * QUART, QUART)

    def piece(slot, core, k):
        return rows_at(slot * HALF + core * QUART + k * PIECE, PIECE)

    def cut(k):
        return slice(k * PIECE, (k + 1) * PIECE)

    feats, proj = (feats_r, feats_p), (proj_r, proj_p)
    local = []

    def load(src, dst):
        copy = pltpu.make_async_copy(src, dst, loc_sem.at[len(local)])
        copy.start()
        local.append(copy)
        return copy

    links = []

    class Link:
        def __init__(self, copy):
            self.copy, self.waited = copy, False

        def start(self):
            self.copy.start()

        def wait_recv(self):
            self.waited = True
            self.copy.wait_recv()

    def remote(src, dst, to, start=True):
        k = len(links)
        link = Link(
            pltpu.make_async_remote_copy(
                src_ref=src, dst_ref=dst, send_sem=send_sem.at[k], recv_sem=recv_sem.at[k],
                device_id=to, device_id_type=pl.DeviceIdType.MESH,
            )
        )
        if start:
            link.start()
        links.append(link)
        return link

    def close():
        for link in links:
            if not link.waited:
                link.copy.wait_recv()
            link.copy.wait_send()

    own_feat = [load(feats[w], fcols.at[w]) for w in (0, 1)]
    own_proj = [load(proj[w], projs.at[w, 0]) for w in (0, 1)]
    own_teach = [load(teach.at[quarter(hh, c)], traw.at[hh]) for hh in (0, 1)]
    own_valid = load(valid, vcols.at[1])

    def own_sum(w):
        own_proj[w].wait()
        part_sum[w] = dot(frows[w, rows_at((1 - h) * HALF, HALF)], projs[w, 0])
        sib_send[w] = part_sum[w, part(1 - c)].astype(BF)

    for w in (0, 1):
        own_feat[w].wait()
        frows[w] = fcols[w].astype(F32).T.astype(BF)
        if w == 0:
            own_sum(0)
    pl.semaphore_wait(barrier, len(peers))

    sum_sib, to_sib, feat_near, feat_nearx, partial = [], [], [], [], []

    def enter(w):
        sum_sib.append(remote(sib_send.at[w], sib_recv.at[w], SIB))
        feat_near.append(remote(frows.at[w, quarter(h, c)], feat_n.at[w, 0], NEAR))
        feat_nearx.append(remote(frows.at[w, quarter(h, 1 - c)], feat_n.at[w, 1], NEARX))

    enter(0)
    own_sum(1)
    enter(1)
    for w in (0, 1):
        sum_sib[w].wait_recv()
        fsend[w] = (part_sum[w, part(c)] + sib_recv[w].astype(F32)).astype(BF)
        partial.append(remote(fsend.at[w], frecv.at[w], FAR))
        to_sib.append(remote(proj[w], projs.at[w, 1], SIB))

    for copy in own_teach:
        copy.wait()
    early = lax.broadcasted_iota(jnp.int32, (1, ROWS), 1) < HALF

    def steps_of(hh, s):
        a = traw[hh, :, s * ROWS:(s + 1) * ROWS].astype(F32)
        d = traw[hh, :, (s + 2) * ROWS:(s + 3) * ROWS].astype(F32)
        keep = jnp.where(h == 0, a, d)
        turn = pltpu.roll(jnp.where(h == 0, d, a), HALF, 1)
        lanes = lax.broadcasted_iota(jnp.int32, (QUART, ROWS), 1)
        return jnp.where((lanes < HALF) == (h == 0), keep, turn)

    for p in (0, 1):
        for hh in (0, 1):
            tsend[p, hh * QUART:(hh + 1) * QUART] = steps_of(hh, 4 * p).astype(BF)
    teach_near = remote(tsend, trecv, NEAR)
    valid_near = remote(valid, vcols.at[0], NEAR)
    for p in (0, 1):
        for hh in (0, 1):
            target[1, p, hh * QUART:(hh + 1) * QUART] = sigmoid(steps_of(hh, 4 * p + 1) / 32.0)
    gr[4 * HALF:] = jnp.zeros((HALF, EMB), F32)

    def finish(w):
        to_sib[w].wait_recv()
        feat_near[w].wait_recv()
        feat_nearx[w].wait_recv()
        pre = dot(feat_n[w, 0], projs[w, 0]) + dot(feat_n[w, 1], projs[w, 1])
        partial[w].wait_recv()
        pre = pre + frecv[w].astype(F32)
        length = jnp.sqrt(jnp.sum(pre * pre, axis=1, keepdims=True) + 1e-06)
        norm[w] = jnp.broadcast_to(length, (QUART, 128))
        u = pre / length
        unit[w] = u
        return u.astype(BF)

    pieces = range(ROWS // 4 // PIECE)
    up_from, down_from, pair_from = (y // 3) * 4, ((y + 3) // 4) * 4, 1 + 2 * odd

    def relay(src, dst, to, start=True):
        return [
            remote(emb_r.at[piece(src, c, k)], emb_r.at[piece(dst, c, k)], to, start)
            for k in pieces
        ]

    def resp_over(slot):
        at = quarter(slot, c)
        return remote(emb_r.at[at], emb_r.at[at], SIB)

    emb_r[part(c)] = finish(0)
    zhop = relay(0, 4, AHEAD)
    up, down = relay(up_from, 1, UP, False), relay(down_from, 3, DOWN, False)
    pair = relay(pair_from, 2, PAIR, False)

    @pl.when(y < 3)
    def _():
        for link in up:
            link.start()

    @pl.when(y == 0)
    def _():
        for link in down:
            link.start()

    resp_sib = [None] * SLOTS
    resp_sib[0] = resp_over(0)

    def zrelay(k):
        zhop[k].wait_recv()

        @pl.when(y == 3)
        def _():
            up[k].start()

        @pl.when(y > 0)
        def _():
            down[k].start()

    zrelay(0)
    emb_p[0, part(h)] = finish(1)
    p_far, p_near, p_opp = [], [], []
    for k in pieces:
        at = rows_at(h * QUART + k * PIECE, PIECE)
        p_far.append(remote(emb_p.at[0, at], emb_p.at[1, at], FAR))
        p_near.append(remote(emb_p.at[0, at], emb_p.at[1, at], NEAR))
    for k in pieces[1:]:
        zrelay(k)
    resp_sib[4] = resp_over(4)

    teach_near.wait_recv()
    for p in (0, 1):
        target[0, p] = sigmoid(trecv[p].astype(F32) / 32.0)
    own_valid.wait()
    valid_near.wait_recv()
    for kind in (0, 1):
        vrows[kind] = vcols[kind].astype(F32).T

    for k in pieces:
        @pl.when(odd == 0)
        def _():
            up[k].wait_recv()

        @pl.when(odd == 1)
        def _():
            down[k].wait_recv()

        pair[k].start()
        p_far[k].wait_recv()
        at = rows_at((1 - h) * QUART + k * PIECE, PIECE)
        p_opp.append(remote(emb_p.at[1, at], emb_p.at[0, at], NEAR))

    for k in pieces:
        @pl.when(odd == 1)
        def _():
            up[k].wait_recv()

        @pl.when(odd == 0)
        def _():
            down[k].wait_recv()

    resp_sib[3], resp_sib[1] = resp_over(3), resp_over(1)
    for k in pieces:
        pair[k].wait_recv()
    resp_sib[2] = resp_over(2)
    for k in pieces:
        p_near[k].wait_recv()
        p_opp[k].wait_recv()
    for i in (4, 3, 2, 1, 0):
        resp_sib[i].wait_recv()

    scale, bias = scale_ref[0], bias_ref[0]
    loss = jnp.zeros((8, ROWS), F32)

    def met(kind, p):
        return pl.ds(pl.multiple_of((2 * p + kind * (1 - l)) * HALF, 64), ROWS)

    for p in (1, 0):
        for kind in (0, 1):
            slots = met(kind, p)
            step = 4 * p + kind
            weight = jnp.concatenate(
                [
                    jnp.where(
                        early,
                        vrows[kind, quarter(hh, c), step:step + 1],
                        vrows[kind, quarter(hh, c), step + 2:step + 3],
                    )
                    for hh in (0, 1)
                ],
                axis=0,
            )
            goal = target[kind, p]
            z = scale * dot(emb_p[kind], emb_r[slots], NT) + bias
            e = jnp.exp(-jnp.abs(z))
            soft = jnp.maximum(z, 0.0) + jnp.log1p(e)
            sig = jnp.where(z >= 0, 1.0, e) / (1.0 + e)
            cost = weight * (soft - goal * z)
            loss = loss + jnp.sum(cost.reshape(HALF // 8, 8, ROWS), axis=0)
            coef = (scale * weight * (sig - goal)).astype(BF)
            coefs[kind, p] = coef
            term_r = dot(coef, emb_p[kind], TN)
            if kind == 0:
                gr[slots] = term_r
            else:
                gr[slots] += term_r

    gathers = []

    def gather(value, me, total, peer_of):
        stage = len(gathers)
        lmsg[stage] = value
        lbuf[stage, me] = value
        gathers.append(
            [remote(lmsg.at[stage], lbuf.at[stage, me], peer_of(k)) for k in range(1, total)]
        )

    def gathered(stage, total):
        for copy in gathers[stage]:
            copy.wait_recv()
        return jnp.sum(lbuf[stage, :total], axis=0)

    gr_sib = [None] * SLOTS

    def push(i):
        grsib_s[i] = gr[quarter(i, 1 - c)].astype(BF)
        gr_sib[i] = remote(grsib_s.at[i], grsib_r.at[i], SIB)

    def join(i):
        gr_sib[i].wait_recv()
        gr[quarter(i, c)] += grsib_r[i].astype(F32)

    def hop(i, to):
        return [
            remote(grsend.at[i, cut(k)], grrecv.at[i, cut(k)], to, False) for k in pieces
        ]

    def fill(i, k):
        grsend[i, cut(k)] = gr[piece(i, c, k)].astype(BF)

    def add(slot, i, k):
        gr[piece(slot, c, k)] += grrecv[i, cut(k)].astype(F32)

    for i in (2, 1, 3, 4, 0):
        push(i)
    for kind in (0, 1):
        gp[kind] = dot(coefs[kind, 0], emb_r[met(kind, 0)]) + dot(coefs[kind, 1], emb_r[met(kind, 1)])
        if kind == 0:
            gpsend[0] = gp[0, part(1 - h)].astype(BF)
            g_opp = [
                remote(gpsend.at[0, cut(k)], gprecv.at[0, cut(k)], NEAR) for k in pieces
            ]
    home_pair, home_down, home_up, home_z = hop(2, PAIR), hop(1, DOWN), hop(3, UP), hop(4, BEHIND)
    join(2)
    for k in pieces:
        fill(2, k)
        home_pair[k].start()
    join(1)
    join(3)

    @pl.when(odd == 0)
    def _():
        for k in pieces:
            fill(3, k)
            home_up[k].start()

    @pl.when(odd == 1)
    def _():
        for k in pieces:
            fill(1, k)
            home_down[k].start()

    lanes = [loss[:, 128 * i:128 * (i + 1)] for i in range(ROWS // 128)]
    gather(lanes[0] + lanes[1] + lanes[2], group_id, 8, group_peer)
    gpsend[1] = gp[1, part(h)].astype(BF)
    join(4)
    join(0)
    g_far, g_near = [], []
    for k in pieces:
        home_pair[k].wait_recv()
        add(pair_from, 2, k)

        @pl.when(odd == 0)
        def _():
            fill(1, k)
            home_down[k].start()

        @pl.when(odd == 1)
        def _():
            fill(3, k)
            home_up[k].start()

        g_opp[k].wait_recv()
        at = rows_at((1 - h) * QUART + k * PIECE, PIECE)
        gpsend[2, cut(k)] = (gp[1, at] + gprecv[0, cut(k)].astype(F32)).astype(BF)
        g_far.append(remote(gpsend.at[2, cut(k)], gprecv.at[2, cut(k)], FAR))
        g_near.append(remote(gpsend.at[1, cut(k)], gprecv.at[1, cut(k)], NEAR))

    gather(gathered(0, 8), y, 4, y_peer)

    d_far, d_sib, o_near, o_nearx = [[], []], [[], []], [None] * 2, [None] * 2

    def back(w, k, g):
        u = unit[w, cut(k)]
        inner = jnp.sum(u * g, axis=1, keepdims=True)
        dsend[w, cut(k)] = ((g - u * inner) / norm[w, cut(k), 0:1]).astype(BF)
        d_far[w].append(remote(dsend.at[w, cut(k)], dbuf.at[w, piece(0, c, k)], FAR))

    def product(w):
        d = dsend[w]
        osend[w, 0] = dot(d, projs[w, 0], NT).astype(BF)
        osend[w, 1] = dot(d, projs[w, 1], NT).astype(BF)
        o_near[w] = remote(osend.at[w, 0], onear.at[w, part(c)], NEAR)
        o_nearx[w] = remote(osend.at[w, 1], onear.at[w, part(c)], NEARX)

    def forward(w):
        for k in pieces:
            d_far[w][k].wait_recv()
            at = piece(0, c, k)
            d_sib[w].append(remote(dbuf.at[w, at], dbuf.at[w, at], SIB))

    for k in pieces:
        home_down[k].wait_recv()
        add(up_from, 1, k)
        home_up[k].wait_recv()
        add(down_from, 3, k)
        fill(4, k)
        home_z[k].start()
        g_near[k].wait_recv()
        g_far[k].wait_recv()
        at = rows_at(h * QUART + k * PIECE, PIECE)
        back(1, k, gp[0, at] + gprecv[1, cut(k)].astype(F32) + gprecv[2, cut(k)].astype(F32))
    gather(gathered(1, 4), b // 8, 8, z_peer)
    for k in pieces:
        home_z[k].wait_recv()
        back(0, k, gr[piece(0, c, k)] + grrecv[4, cut(k)].astype(F32))
    product(1)
    product(0)
    forward(1)

    outs = (out_r, out_p)

    def place(w, half, block):
        @pl.when(half == 0)
        def _():
            oval[w, :, :HALF] = block

        @pl.when(half == 1)
        def _():
            oval[w, :, HALF:] = block

    written = []
    for w in (1, 0):
        if w == 0:
            forward(0)
        o_near[w].wait_recv()
        o_nearx[w].wait_recv()
        place(w, h, onear[w].astype(F32).T.astype(BF))
        for link in d_sib[w]:
            link.wait_recv()
        place(w, 1 - h, dot(projs[w, 0], dbuf[w], NT).astype(BF))
        written.append(load(oval.at[w], outs[w]))
    loss_ref[0] = jnp.sum(gathered(2, 8)) / (ROWS * BLOCKS * STEPS * ROWS)
    for copy in written:
        copy.wait()
    close()


def on_device(
    prompt_feats, response_feats, prompt_proj, response_proj,
    logit_scale, logit_bias, teacher, valid,
):
    anywhere = pl.BlockSpec(memory_space=pl.ANY)
    scalar = pl.BlockSpec(memory_space=pltpu.SMEM)

    def vm(*shape, kind=BF):
        return pltpu.VMEM(shape, kind)

    grad_response, grad_prompt, loss = pl.pallas_call(
        kernel,
        out_shape=(
            jax.ShapeDtypeStruct((FEAT, ROWS), BF),
            jax.ShapeDtypeStruct((FEAT, ROWS), BF),
            jax.ShapeDtypeStruct((1,), F32),
        ),
        in_specs=[anywhere] * 4 + [scalar] * 2 + [anywhere] * 2,
        out_specs=(anywhere, anywhere, scalar),
        scratch_shapes=[
            vm(2, FEAT, ROWS),
            vm(2, ROWS, FEAT),
            vm(2, 2, FEAT, EMB),
            vm(2, HALF, EMB, kind=F32),
            vm(2, QUART, EMB),
            vm(2, QUART, EMB),
            vm(2, 2, QUART, FEAT),
            vm(2, QUART, EMB),
            vm(2, QUART, EMB),
            vm(2, QUART, EMB, kind=F32),
            vm(2, QUART, 128, kind=F32),
            vm(2, HALF, EMB),
            vm(SLOTS * HALF, EMB),
            vm(2, QUART, STEPS * ROWS, kind=jnp.int32),
            vm(2, HALF, ROWS),
            vm(2, HALF, ROWS),
            vm(2, 2, HALF, ROWS, kind=F32),
            vm(2, STEPS, ROWS, kind=jnp.int32),
            vm(2, ROWS, STEPS, kind=F32),
            vm(2, 2, HALF, ROWS),
            vm(2, HALF, EMB, kind=F32),
            vm(SLOTS * HALF, EMB, kind=F32),
            vm(3, QUART, EMB),
            vm(3, QUART, EMB),
            vm(SLOTS, QUART, EMB),
            vm(SLOTS, QUART, EMB),
            vm(SLOTS, QUART, EMB),
            vm(SLOTS, QUART, EMB),
            vm(2, QUART, EMB),
            vm(2, HALF, EMB),
            vm(2, 2, QUART, FEAT),
            vm(2, HALF, FEAT),
            vm(2, FEAT, ROWS),
            vm(3, 8, 128, kind=F32),
            vm(3, 8, 8, 128, kind=F32),
            pltpu.SemaphoreType.DMA((112,)),
            pltpu.SemaphoreType.DMA((112,)),
            pltpu.SemaphoreType.DMA((16,)),
        ],
        compiler_params=pltpu.CompilerParams(
            collective_id=0, has_side_effects=True, vmem_limit_bytes=56 * 2**20
        ),
        name="band",
    )(
        response_feats.T, prompt_feats.T, response_proj, prompt_proj,
        logit_scale, logit_bias, teacher, valid.T,
    )
    return grad_prompt.T, grad_response.T, loss


def solution(mesh):
    in_specs = (
        P("batch", "tower"), P("batch", "tower"), P("tower", None), P("tower", None),
        P(), P(), P("batch", None), P("batch", None),
    )
    out_specs = (P("batch", "tower"), P("batch", "tower"), P())
    return jax.shard_map(
        on_device, mesh=mesh, in_specs=in_specs, out_specs=out_specs, check_vma=False
    )
```

```python
import jax
import jax.numpy as jnp
from jax import lax
from jax.experimental import pallas as pl
from jax.experimental.pallas import tpu as pltpu
from jax.sharding import PartitionSpec as P

BF, F32 = jnp.bfloat16, jnp.float32
ROWS, FEAT, EMB, STEPS, BLOCKS, TOWER = 384, 288, 1152, 8, 64, 4
HALF, QUART = ROWS // 2, ROWS // 4
SLOTS, PIECE = 5, 32
NT = (((1,), (1,)), ((), ()))
TN = (((0,), (0,)), ((), ()))


def dot(a, b, dims=(((1,), (0,)), ((), ()))):
    return lax.dot_general(a, b, dims, preferred_element_type=F32)


def sigmoid(x):
    e = jnp.exp(-jnp.abs(x))
    return jnp.where(x >= 0, 1.0, e) / (1.0 + e)


def kernel(
    feats_r, feats_p, proj_r, proj_p, scale_ref, bias_ref, teach, valid,
    oval, loss_ref,
    fcols, frows, projs, part_sum, sib_send, sib_recv, feat_n, fsend, frecv, unit, norm, emb_p, emb_r,
    traw, tsend, trecv, target, vcols, vrows, coefs, gp, gr, gpsend, gprecv,
    grsib_s, grsib_r, grsend, grrecv, dsend, dbuf, osend, onear,
    lmsg, lbuf, send_sem, recv_sem, loc_sem,
):
    b = lax.axis_index("batch")
    t = lax.axis_index("tower")
    l = lax.rem(b, 2)
    h, c = t // 2, lax.rem(t, 2)
    nb = b + 1 - 2 * l
    st = t + 1 - 2 * c
    ft = lax.rem(t + 2, TOWER)
    plane = (b // 8) * 8
    inplane = b - plane
    y = inplane // 2
    odd = lax.rem(y, 2)

    def dev(batch, tower):
        return {"batch": batch, "tower": tower}

    SIB, NEAR, NEARX, FAR = dev(b, st), dev(nb, t), dev(nb, st), dev(nb, ft)
    UP, DOWN = dev(plane + lax.rem(inplane + 2, 8), t), dev(plane + lax.rem(inplane + 6, 8), t)
    PAIR = dev(b + 2 - 4 * odd, t)
    AHEAD, BEHIND = dev(lax.rem(b + 8, BLOCKS), t), dev(lax.rem(b + BLOCKS - 8, BLOCKS), t)
    group_id = l * TOWER + t

    def group_peer(k):
        g = lax.rem(group_id + k, 8)
        return dev(b - l + g // TOWER, lax.rem(g, TOWER))

    def y_peer(k):
        return dev(plane + lax.rem(inplane + 2 * k, 8), t)

    def z_peer(k):
        return dev(lax.rem(b + 8 * k, BLOCKS), t)

    barrier = pltpu.get_barrier_semaphore()
    peers = [group_peer(k) for k in range(1, 8)]
    peers += [y_peer(k) for k in range(1, 4)] + [z_peer(k) for k in range(1, 8)]
    for peer in peers:
        pl.semaphore_signal(barrier, inc=1, device_id=peer, device_id_type=pl.DeviceIdType.MESH)

    def rows_at(start, count):
        return pl.ds(pl.multiple_of(start, 16), count)

    def quarter(half, core):
        return rows_at(half * HALF + core * QUART, QUART)

    def part(core):
        return rows_at(core * QUART, QUART)

    def piece(slot, core, k):
        return rows_at(slot * HALF + core * QUART + k * PIECE, PIECE)

    def cut(k):
        return slice(k * PIECE, (k + 1) * PIECE)

    feats, proj = (feats_r, feats_p), (proj_r, proj_p)
    local = []

    def load(src, dst):
        copy = pltpu.make_async_copy(src, dst, loc_sem.at[len(local)])
        copy.start()
        local.append(copy)
        return copy

    links = []

    class Link:
        def __init__(self, copy):
            self.copy, self.waited = copy, False

        def start(self):
            self.copy.start()

        def wait_recv(self):
            self.waited = True
            self.copy.wait_recv()

    def remote(src, dst, to, start=True):
        k = len(links)
        link = Link(
            pltpu.make_async_remote_copy(
                src_ref=src, dst_ref=dst, send_sem=send_sem.at[k], recv_sem=recv_sem.at[k],
                device_id=to, device_id_type=pl.DeviceIdType.MESH,
            )
        )
        if start:
            link.start()
        links.append(link)
        return link

    def close():
        for link in links:
            if not link.waited:
                link.copy.wait_recv()
            link.copy.wait_send()

    own_feat = [load(feats[w], fcols.at[w]) for w in (0, 1)]
    own_proj = [load(proj[w], projs.at[w, 0]) for w in (0, 1)]
    own_teach = [load(teach.at[quarter(hh, c)], traw.at[hh]) for hh in (0, 1)]
    own_valid = load(valid, vcols.at[1])

    def own_sum(w):
        own_proj[w].wait()
        part_sum[w] = dot(frows[w, rows_at((1 - h) * HALF, HALF)], projs[w, 0])
        sib_send[w] = part_sum[w, part(1 - c)].astype(BF)

    for w in (0, 1):
        own_feat[w].wait()
        frows[w] = fcols[w].astype(F32).T.astype(BF)
        if w == 0:
            own_sum(0)
    pl.semaphore_wait(barrier, len(peers))

    sum_sib, to_sib, feat_near, feat_nearx, partial = [], [], [], [], []

    def enter(w):
        sum_sib.append(remote(sib_send.at[w], sib_recv.at[w], SIB))
        feat_near.append(remote(frows.at[w, quarter(h, c)], feat_n.at[w, 0], NEAR))
        feat_nearx.append(remote(frows.at[w, quarter(h, 1 - c)], feat_n.at[w, 1], NEARX))

    enter(0)
    own_sum(1)
    enter(1)
    pieces = range(QUART // PIECE)
    for w in (0, 1):
        sum_sib[w].wait_recv()
        fsend[w] = (part_sum[w, part(c)] + sib_recv[w].astype(F32)).astype(BF)
        partial.append(
            [remote(fsend.at[w, cut(k)], frecv.at[w, cut(k)], FAR, w == 0) for k in pieces]
        )
        to_sib.append(remote(proj[w], projs.at[w, 1], SIB))

    for copy in own_teach:
        copy.wait()
    early = lax.broadcasted_iota(jnp.int32, (1, ROWS), 1) < HALF

    def steps_of(hh, s):
        a = traw[hh, :, s * ROWS:(s + 1) * ROWS].astype(F32)
        d = traw[hh, :, (s + 2) * ROWS:(s + 3) * ROWS].astype(F32)
        keep = jnp.where(h == 0, a, d)
        turn = pltpu.roll(jnp.where(h == 0, d, a), HALF, 1)
        lanes = lax.broadcasted_iota(jnp.int32, (QUART, ROWS), 1)
        return jnp.where((lanes < HALF) == (h == 0), keep, turn)

    for p in (0, 1):
        for hh in (0, 1):
            tsend[p, hh * QUART:(hh + 1) * QUART] = steps_of(hh, 4 * p).astype(BF)
    teach_near = remote(tsend, trecv, NEAR)
    valid_near = remote(valid, vcols.at[0], NEAR)
    for p in (0, 1):
        for hh in (0, 1):
            target[1, p, hh * QUART:(hh + 1) * QUART] = sigmoid(steps_of(hh, 4 * p + 1) / 32.0)
    gr[4 * HALF:] = jnp.zeros((HALF, EMB), F32)

    def near_sum(w):
        to_sib[w].wait_recv()
        feat_near[w].wait_recv()
        feat_nearx[w].wait_recv()
        unit[w] = dot(feat_n[w, 0], projs[w, 0]) + dot(feat_n[w, 1], projs[w, 1])

    def finish(w, k):
        pre = unit[w, cut(k)] + frecv[w, cut(k)].astype(F32)
        length = jnp.sqrt(jnp.sum(pre * pre, axis=1, keepdims=True) + 1e-06)
        norm[w, cut(k)] = jnp.broadcast_to(length, (PIECE, 128))
        u = pre / length
        unit[w, cut(k)] = u
        return u.astype(BF)

    up_from, down_from, pair_from = (y // 3) * 4, ((y + 3) // 4) * 4, 1 + 2 * odd

    def relay(src, dst, to):
        return [
            remote(emb_r.at[piece(src, c, k)], emb_r.at[piece(dst, c, k)], to, False)
            for k in pieces
        ]

    def resp_over(slot):
        at = quarter(slot, c)
        return remote(emb_r.at[at], emb_r.at[at], SIB)

    zhop = relay(0, 4, AHEAD)
    up, down = relay(up_from, 1, UP), relay(down_from, 3, DOWN)
    pair = relay(pair_from, 2, PAIR)
    near_sum(0)
    for k in pieces:
        partial[0][k].wait_recv()
        partial[1][k].start()
        emb_r[piece(0, c, k)] = finish(0, k)
        zhop[k].start()

        @pl.when(y < 3)
        def _():
            up[k].start()

        @pl.when(y == 0)
        def _():
            down[k].start()

    resp_sib = [None] * SLOTS
    resp_sib[0] = resp_over(0)

    def zrelay(k):
        zhop[k].wait_recv()

        @pl.when(y == 3)
        def _():
            up[k].start()

        @pl.when(y > 0)
        def _():
            down[k].start()

    near_sum(1)
    p_far, p_near, p_opp = [], [], []
    for k in pieces:
        zrelay(k)
        partial[1][k].wait_recv()
        at = rows_at(h * QUART + k * PIECE, PIECE)
        emb_p[0, at] = finish(1, k)
        p_far.append(remote(emb_p.at[0, at], emb_p.at[1, at], FAR))
        p_near.append(remote(emb_p.at[0, at], emb_p.at[1, at], NEAR))
    resp_sib[4] = resp_over(4)

    teach_near.wait_recv()
    for p in (0, 1):
        target[0, p] = sigmoid(trecv[p].astype(F32) / 32.0)
    own_valid.wait()
    valid_near.wait_recv()
    for kind in (0, 1):
        vrows[kind] = vcols[kind].astype(F32).T

    for k in pieces:
        @pl.when(odd == 0)
        def _():
            up[k].wait_recv()

        @pl.when(odd == 1)
        def _():
            down[k].wait_recv()

        pair[k].start()
        p_far[k].wait_recv()
        at = rows_at((1 - h) * QUART + k * PIECE, PIECE)
        p_opp.append(remote(emb_p.at[1, at], emb_p.at[0, at], NEAR))

    for k in pieces:
        @pl.when(odd == 1)
        def _():
            up[k].wait_recv()

        @pl.when(odd == 0)
        def _():
            down[k].wait_recv()

    resp_sib[3], resp_sib[1] = resp_over(3), resp_over(1)
    for k in pieces:
        pair[k].wait_recv()
    resp_sib[2] = resp_over(2)
    for k in pieces:
        p_near[k].wait_recv()
        p_opp[k].wait_recv()
    for i in (4, 3, 2, 1, 0):
        resp_sib[i].wait_recv()

    def push(i):
        grsib_s[i] = gr[quarter(i, 1 - c)].astype(BF)
        return remote(grsib_s.at[i], grsib_r.at[i], SIB)

    def join(i, link):
        link.wait_recv()
        gr[quarter(i, c)] += grsib_r[i].astype(F32)

    def hop(i, to):
        return [
            remote(grsend.at[i, cut(k)], grrecv.at[i, cut(k)], to, False) for k in pieces
        ]

    def fill(i, k):
        grsend[i, cut(k)] = gr[piece(i, c, k)].astype(BF)

    def add(slot, i, k):
        gr[piece(slot, c, k)] += grrecv[i, cut(k)].astype(F32)

    home_pair, home_down, home_up, home_z = hop(2, PAIR), hop(1, DOWN), hop(3, UP), hop(4, BEHIND)

    def send_soon():
        @pl.when(odd == 0)
        def _():
            for k in pieces:
                fill(3, k)
                home_up[k].start()

        @pl.when(odd == 1)
        def _():
            for k in pieces:
                fill(1, k)
                home_down[k].start()

    scale, bias = scale_ref[0], bias_ref[0]
    loss = jnp.zeros((8, ROWS), F32)

    def met(kind, p):
        return pl.ds(pl.multiple_of((2 * p + kind * (1 - l)) * HALF, 64), ROWS)

    soon = 4 - pair_from
    for p in (1, 0):
        for kind in (0, 1):
            slots = met(kind, p)

            def column(hh, s):
                at = 4 * p + s
                return vrows[kind, quarter(hh, c), at:at + 1]

            weight = jnp.concatenate(
                [jnp.where(early, column(hh, kind), column(hh, kind + 2)) for hh in (0, 1)], axis=0
            )
            goal = target[kind, p]
            z = scale * dot(emb_p[kind], emb_r[slots], NT) + bias
            e = jnp.exp(-jnp.abs(z))
            soft = jnp.maximum(z, 0.0) + jnp.log1p(e)
            sig = jnp.where(z >= 0, 1.0, e) / (1.0 + e)
            cost = weight * (soft - goal * z)
            loss = loss + jnp.sum(cost.reshape(HALF // 8, 8, ROWS), axis=0)
            coef = (scale * weight * (sig - goal)).astype(BF)
            coefs[kind, p] = coef
            term_r = dot(coef, emb_p[kind], TN)
            if kind == 0:
                gr[slots] = term_r
            else:
                gr[slots] += term_r

    gathers = []

    def gather(value, me, total, peer_of):
        stage = len(gathers)
        lmsg[stage] = value
        lbuf[stage, me] = value
        gathers.append(
            [remote(lmsg.at[stage], lbuf.at[stage, me], peer_of(k)) for k in range(1, total)]
        )

    def gathered(stage, total):
        for copy in gathers[stage]:
            copy.wait_recv()
        return jnp.sum(lbuf[stage, :total], axis=0)

    sib_pair, sib_soon, sib_late, sib_four, sib_zero = [push(i) for i in (2, soon, pair_from, 4, 0)]
    for kind in (0, 1):
        gp[kind] = dot(coefs[kind, 0], emb_r[met(kind, 0)]) + dot(coefs[kind, 1], emb_r[met(kind, 1)])
        if kind == 0:
            gpsend[0] = gp[0, part(1 - h)].astype(BF)
            g_opp = [
                remote(gpsend.at[0, cut(k)], gprecv.at[0, cut(k)], NEAR) for k in pieces
            ]
    join(2, sib_pair)
    for k in pieces:
        fill(2, k)
        home_pair[k].start()
    join(soon, sib_soon)
    send_soon()
    join(pair_from, sib_late)
    lanes = [loss[:, 128 * i:128 * (i + 1)] for i in range(ROWS // 128)]
    gather(lanes[0] + lanes[1] + lanes[2], group_id, 8, group_peer)
    gpsend[1] = gp[1, part(h)].astype(BF)
    join(4, sib_four)
    join(0, sib_zero)
    g_far, g_near = [], []
    for k in pieces:
        home_pair[k].wait_recv()
        add(pair_from, 2, k)

        @pl.when(odd == 0)
        def _():
            fill(1, k)
            home_down[k].start()

        @pl.when(odd == 1)
        def _():
            fill(3, k)
            home_up[k].start()

        g_opp[k].wait_recv()
        at = rows_at((1 - h) * QUART + k * PIECE, PIECE)
        gpsend[2, cut(k)] = (gp[1, at] + gprecv[0, cut(k)].astype(F32)).astype(BF)
        g_far.append(remote(gpsend.at[2, cut(k)], gprecv.at[2, cut(k)], FAR))
        g_near.append(remote(gpsend.at[1, cut(k)], gprecv.at[1, cut(k)], NEAR))

    gather(gathered(0, 8), y, 4, y_peer)

    d_far, d_sib, o_near, o_nearx = [[], []], [[], []], [None] * 2, [None] * 2

    def back(w, k, g):
        u = unit[w, cut(k)]
        inner = jnp.sum(u * g, axis=1, keepdims=True)
        dsend[w, cut(k)] = ((g - u * inner) / norm[w, cut(k), 0:1]).astype(BF)
        d_far[w].append(remote(dsend.at[w, cut(k)], dbuf.at[w, piece(0, c, k)], FAR))

    def product(w):
        d = dsend[w]
        osend[w, 0] = dot(d, projs[w, 0], NT).astype(BF)
        osend[w, 1] = dot(d, projs[w, 1], NT).astype(BF)
        o_near[w] = remote(osend.at[w, 0], onear.at[w, part(c)], NEAR)
        o_nearx[w] = remote(osend.at[w, 1], onear.at[w, part(c)], NEARX)

    def forward(w):
        for k in pieces:
            d_far[w][k].wait_recv()
            at = piece(0, c, k)
            d_sib[w].append(remote(dbuf.at[w, at], dbuf.at[w, at], SIB))

    for k in pieces:
        home_down[k].wait_recv()
        add(up_from, 1, k)
        home_up[k].wait_recv()
        add(down_from, 3, k)
        fill(4, k)
        home_z[k].start()
        g_near[k].wait_recv()
        g_far[k].wait_recv()
        at = rows_at(h * QUART + k * PIECE, PIECE)
        back(1, k, gp[0, at] + gprecv[1, cut(k)].astype(F32) + gprecv[2, cut(k)].astype(F32))
    gather(gathered(1, 4), b // 8, 8, z_peer)
    for k in pieces:
        home_z[k].wait_recv()
        back(0, k, gr[piece(0, c, k)] + grrecv[4, cut(k)].astype(F32))
    product(1)
    product(0)
    forward(1)

    def place(w, half, block):
        @pl.when(half == 0)
        def _():
            oval[w, :, :HALF] = block

        @pl.when(half == 1)
        def _():
            oval[w, :, HALF:] = block

    for w in (1, 0):
        if w == 0:
            forward(0)
        o_near[w].wait_recv()
        o_nearx[w].wait_recv()
        place(w, h, onear[w].astype(F32).T.astype(BF))
        for link in d_sib[w]:
            link.wait_recv()
        place(w, 1 - h, dot(projs[w, 0], dbuf[w], NT).astype(BF))
    loss_ref[0] = jnp.sum(gathered(2, 8)) / (ROWS * BLOCKS * STEPS * ROWS)
    close()


def deliver(grads, out_r, out_p, sem):
    copies = [pltpu.make_async_copy(grads.at[w], (out_r, out_p)[w], sem.at[w]) for w in (0, 1)]
    for copy in copies:
        copy.start()
    for copy in copies:
        copy.wait()


def on_device(
    prompt_feats, response_feats, prompt_proj, response_proj,
    logit_scale, logit_bias, teacher, valid,
):
    anywhere = pl.BlockSpec(memory_space=pl.ANY)
    scalar = pl.BlockSpec(memory_space=pltpu.SMEM)

    def vm(*shape, kind=BF):
        return pltpu.VMEM(shape, kind)

    grads, loss = pl.pallas_call(
        kernel,
        out_shape=(
            pltpu.VMEM((2, FEAT, ROWS), BF),
            jax.ShapeDtypeStruct((1,), F32),
        ),
        in_specs=[anywhere] * 4 + [scalar] * 2 + [anywhere] * 2,
        out_specs=(pl.BlockSpec(memory_space=pltpu.VMEM), scalar),
        scratch_shapes=[
            vm(2, FEAT, ROWS),
            vm(2, ROWS, FEAT),
            vm(2, 2, FEAT, EMB),
            vm(2, HALF, EMB, kind=F32),
            vm(2, QUART, EMB),
            vm(2, QUART, EMB),
            vm(2, 2, QUART, FEAT),
            vm(2, QUART, EMB),
            vm(2, QUART, EMB),
            vm(2, QUART, EMB, kind=F32),
            vm(2, QUART, 128, kind=F32),
            vm(2, HALF, EMB),
            vm(SLOTS * HALF, EMB),
            vm(2, QUART, STEPS * ROWS, kind=jnp.int32),
            vm(2, HALF, ROWS),
            vm(2, HALF, ROWS),
            vm(2, 2, HALF, ROWS, kind=F32),
            vm(2, STEPS, ROWS, kind=jnp.int32),
            vm(2, ROWS, STEPS, kind=F32),
            vm(2, 2, HALF, ROWS),
            vm(2, HALF, EMB, kind=F32),
            vm(SLOTS * HALF, EMB, kind=F32),
            vm(3, QUART, EMB),
            vm(3, QUART, EMB),
            vm(SLOTS, QUART, EMB),
            vm(SLOTS, QUART, EMB),
            vm(SLOTS, QUART, EMB),
            vm(SLOTS, QUART, EMB),
            vm(2, QUART, EMB),
            vm(2, HALF, EMB),
            vm(2, 2, QUART, FEAT),
            vm(2, HALF, FEAT),
            vm(3, 8, 128, kind=F32),
            vm(3, 8, 8, 128, kind=F32),
            pltpu.SemaphoreType.DMA((128,)),
            pltpu.SemaphoreType.DMA((128,)),
            pltpu.SemaphoreType.DMA((16,)),
        ],
        compiler_params=pltpu.CompilerParams(
            collective_id=0, has_side_effects=True, vmem_limit_bytes=56 * 2**20
        ),
        name="band",
    )(
        response_feats.T, prompt_feats.T, response_proj, prompt_proj,
        logit_scale, logit_bias, teacher, valid.T,
    )
    grad_response, grad_prompt = pl.pallas_call(
        deliver,
        out_shape=(jax.ShapeDtypeStruct((FEAT, ROWS), BF),) * 2,
        in_specs=[pl.BlockSpec(memory_space=pltpu.VMEM)],
        out_specs=(anywhere, anywhere),
        scratch_shapes=[pltpu.SemaphoreType.DMA((2,))],
        name="deliver",
    )(pltpu.with_memory_space_constraint(grads, pltpu.VMEM))
    return grad_prompt.T, grad_response.T, loss


def solution(mesh):
    in_specs = (
        P("batch", "tower"), P("batch", "tower"), P("tower", None), P("tower", None),
        P(), P(), P("batch", None), P("batch", None),
    )
    out_specs = (P("batch", "tower"), P("batch", "tower"), P())
    return jax.shard_map(
        on_device, mesh=mesh, in_specs=in_specs, out_specs=out_specs, check_vma=False
    )
```

```python
import jax
import jax.numpy as jnp
from jax import lax
from jax.experimental import pallas as pl
from jax.experimental.pallas import tpu as pltpu
from jax.sharding import PartitionSpec as P

BF, F32 = jnp.bfloat16, jnp.float32
ROWS, FEAT, EMB, STEPS, BLOCKS, TOWER = 384, 288, 1152, 8, 64, 4
HALF, QUART = ROWS // 2, ROWS // 4
SLOTS, PIECE = 5, 32
NT = (((1,), (1,)), ((), ()))
TN = (((0,), (0,)), ((), ()))


def dot(a, b, dims=(((1,), (0,)), ((), ()))):
    return lax.dot_general(a, b, dims, preferred_element_type=F32)


def sigmoid(x):
    e = jnp.exp(-jnp.abs(x))
    return jnp.where(x >= 0, 1.0, e) / (1.0 + e)


def kernel(
    feats_r, feats_p, proj_r, proj_p, scale_ref, bias_ref, teach, valid,
    oval, loss_ref,
    fcols, frows, projs, part_sum, sib_send, sib_recv, feat_n, fsend, frecv, unit, norm, emb_p, emb_r,
    traw, tsend, trecv, target, vcols, vrows, coefs, gp, gr, gpsend, gprecv,
    grsib_s, grsib_r, grsend, grrecv, dsend, dbuf, osend, onear,
    lmsg, lbuf, send_sem, recv_sem, loc_sem,
):
    b = lax.axis_index("batch")
    t = lax.axis_index("tower")
    l = lax.rem(b, 2)
    h, c = t // 2, lax.rem(t, 2)
    nb = b + 1 - 2 * l
    st = t + 1 - 2 * c
    ft = lax.rem(t + 2, TOWER)
    plane = (b // 8) * 8
    inplane = b - plane
    y = inplane // 2
    odd = lax.rem(y, 2)

    def dev(batch, tower):
        return {"batch": batch, "tower": tower}

    SIB, NEAR, NEARX, FAR = dev(b, st), dev(nb, t), dev(nb, st), dev(nb, ft)
    UP, DOWN = dev(plane + lax.rem(inplane + 2, 8), t), dev(plane + lax.rem(inplane + 6, 8), t)
    PAIR = dev(b + 2 - 4 * odd, t)
    AHEAD, BEHIND = dev(lax.rem(b + 8, BLOCKS), t), dev(lax.rem(b + BLOCKS - 8, BLOCKS), t)
    group_id = l * TOWER + t

    def group_peer(k):
        g = lax.rem(group_id + k, 8)
        return dev(b - l + g // TOWER, lax.rem(g, TOWER))

    def y_peer(k):
        return dev(plane + lax.rem(inplane + 2 * k, 8), t)

    def z_peer(k):
        return dev(lax.rem(b + 8 * k, BLOCKS), t)

    barrier = pltpu.get_barrier_semaphore()
    peers = [group_peer(k) for k in range(1, 8)]
    peers += [y_peer(k) for k in range(1, 4)] + [z_peer(k) for k in range(1, 8)]
    for peer in peers:
        pl.semaphore_signal(barrier, inc=1, device_id=peer, device_id_type=pl.DeviceIdType.MESH)

    def rows_at(start, count):
        return pl.ds(pl.multiple_of(start, 16), count)

    def quarter(half, core):
        return rows_at(half * HALF + core * QUART, QUART)

    def part(core):
        return rows_at(core * QUART, QUART)

    def piece(slot, core, k):
        return rows_at(slot * HALF + core * QUART + k * PIECE, PIECE)

    def cut(k):
        return slice(k * PIECE, (k + 1) * PIECE)

    feats, proj = (feats_r, feats_p), (proj_r, proj_p)
    local = []

    def load(src, dst):
        copy = pltpu.make_async_copy(src, dst, loc_sem.at[len(local)])
        copy.start()
        local.append(copy)
        return copy

    links = []

    class Link:
        def __init__(self, copy):
            self.copy, self.waited, self.sent = copy, False, False

        def start(self):
            self.copy.start()

        def wait_recv(self):
            self.waited = True
            self.copy.wait_recv()

    def remote(src, dst, to, start=True):
        k = len(links)
        link = Link(
            pltpu.make_async_remote_copy(
                src_ref=src, dst_ref=dst, send_sem=send_sem.at[k], recv_sem=recv_sem.at[k],
                device_id=to, device_id_type=pl.DeviceIdType.MESH,
            )
        )
        if start:
            link.start()
        links.append(link)
        return link

    def settle(some):
        for link in some:
            if not link.sent:
                link.sent = True
                link.copy.wait_send()

    own_feat = [load(feats[w], fcols.at[w]) for w in (0, 1)]
    own_proj = [load(proj[w], projs.at[w, 0]) for w in (0, 1)]
    own_teach = [load(teach.at[quarter(hh, c)], traw.at[hh]) for hh in (0, 1)]
    own_valid = load(valid, vcols.at[1])

    def own_sum(w):
        own_proj[w].wait()
        part_sum[w] = dot(frows[w, rows_at((1 - h) * HALF, HALF)], projs[w, 0])
        sib_send[w] = part_sum[w, part(1 - c)].astype(BF)

    for w in (0, 1):
        own_feat[w].wait()
        frows[w] = fcols[w].astype(F32).T.astype(BF)
        if w == 0:
            own_sum(0)
    pl.semaphore_wait(barrier, len(peers))

    sum_sib, to_sib, feat_near, feat_nearx, partial = [], [], [], [], []

    def enter(w):
        sum_sib.append(remote(sib_send.at[w], sib_recv.at[w], SIB))
        feat_near.append(remote(frows.at[w, quarter(h, c)], feat_n.at[w, 0], NEAR))
        feat_nearx.append(remote(frows.at[w, quarter(h, 1 - c)], feat_n.at[w, 1], NEARX))

    enter(0)
    own_sum(1)
    enter(1)
    pieces = range(QUART // PIECE)
    for w in (0, 1):
        sum_sib[w].wait_recv()
        fsend[w] = (part_sum[w, part(c)] + sib_recv[w].astype(F32)).astype(BF)
        partial.append(
            [remote(fsend.at[w, cut(k)], frecv.at[w, cut(k)], FAR, w == 0) for k in pieces]
        )
        to_sib.append(remote(proj[w], projs.at[w, 1], SIB))

    for copy in own_teach:
        copy.wait()
    early = lax.broadcasted_iota(jnp.int32, (1, ROWS), 1) < HALF

    def steps_of(hh, s):
        a = traw[hh, :, s * ROWS:(s + 1) * ROWS].astype(F32)
        d = traw[hh, :, (s + 2) * ROWS:(s + 3) * ROWS].astype(F32)
        keep = jnp.where(h == 0, a, d)
        turn = pltpu.roll(jnp.where(h == 0, d, a), HALF, 1)
        lanes = lax.broadcasted_iota(jnp.int32, (QUART, ROWS), 1)
        return jnp.where((lanes < HALF) == (h == 0), keep, turn)

    for p in (0, 1):
        for hh in (0, 1):
            tsend[p, hh * QUART:(hh + 1) * QUART] = steps_of(hh, 4 * p).astype(BF)
    teach_near = remote(tsend, trecv, NEAR)
    valid_near = remote(valid, vcols.at[0], NEAR)
    for p in (0, 1):
        for hh in (0, 1):
            target[1, p, hh * QUART:(hh + 1) * QUART] = sigmoid(steps_of(hh, 4 * p + 1) / 32.0)
    for i in (0, 4):
        gr[i * HALF:(i + 1) * HALF] = jnp.zeros((HALF, EMB), F32)

    def near_sum(w):
        to_sib[w].wait_recv()
        feat_near[w].wait_recv()
        feat_nearx[w].wait_recv()
        unit[w] = dot(feat_n[w, 0], projs[w, 0]) + dot(feat_n[w, 1], projs[w, 1])

    def finish(w, k):
        pre = unit[w, cut(k)] + frecv[w, cut(k)].astype(F32)
        length = jnp.sqrt(jnp.sum(pre * pre, axis=1, keepdims=True) + 1e-06)
        norm[w, cut(k)] = jnp.broadcast_to(length, (PIECE, 128))
        u = pre / length
        unit[w, cut(k)] = u
        return u.astype(BF)

    up_from, down_from, pair_from = (y // 3) * 4, ((y + 3) // 4) * 4, 1 + 2 * odd

    def relay(src, dst, to):
        return [
            remote(emb_r.at[piece(src, c, k)], emb_r.at[piece(dst, c, k)], to, False)
            for k in pieces
        ]

    def resp_over(slot):
        at = quarter(slot, c)
        return remote(emb_r.at[at], emb_r.at[at], SIB)

    zhop = relay(0, 4, AHEAD)
    up, down = relay(up_from, 1, UP), relay(down_from, 3, DOWN)
    pair = relay(pair_from, 2, PAIR)
    near_sum(0)
    for k in pieces:
        partial[0][k].wait_recv()
        partial[1][k].start()
        emb_r[piece(0, c, k)] = finish(0, k)
        zhop[k].start()

        @pl.when(y < 3)
        def _():
            up[k].start()

        @pl.when(y == 0)
        def _():
            down[k].start()

    resp_sib = [None] * SLOTS
    resp_sib[0] = resp_over(0)

    def zrelay(k):
        zhop[k].wait_recv()

        @pl.when(y == 3)
        def _():
            up[k].start()

        @pl.when(y > 0)
        def _():
            down[k].start()

    near_sum(1)
    p_far, p_near, p_opp = [], [], []
    for k in pieces:
        zrelay(k)
        partial[1][k].wait_recv()
        at = rows_at(h * QUART + k * PIECE, PIECE)
        emb_p[0, at] = finish(1, k)
        p_far.append(remote(emb_p.at[0, at], emb_p.at[1, at], FAR))
        p_near.append(remote(emb_p.at[0, at], emb_p.at[1, at], NEAR))
    resp_sib[4] = resp_over(4)

    teach_near.wait_recv()
    for p in (0, 1):
        target[0, p] = sigmoid(trecv[p].astype(F32) / 32.0)
    own_valid.wait()
    valid_near.wait_recv()
    for kind in (0, 1):
        vrows[kind] = vcols[kind].astype(F32).T

    for k in pieces:
        @pl.when(odd == 0)
        def _():
            up[k].wait_recv()

        @pl.when(odd == 1)
        def _():
            down[k].wait_recv()

        pair[k].start()
        p_far[k].wait_recv()
        at = rows_at((1 - h) * QUART + k * PIECE, PIECE)
        p_opp.append(remote(emb_p.at[1, at], emb_p.at[0, at], NEAR))

    for k in pieces:
        @pl.when(odd == 1)
        def _():
            up[k].wait_recv()

        @pl.when(odd == 0)
        def _():
            down[k].wait_recv()

    resp_sib[3], resp_sib[1] = resp_over(3), resp_over(1)
    resp_two = []
    for k in pieces:
        pair[k].wait_recv()
        at = piece(2, c, k)
        resp_two.append(remote(emb_r.at[at], emb_r.at[at], SIB))
    for k in pieces:
        p_near[k].wait_recv()
    for link in [resp_sib[i] for i in (4, 3, 1, 0)] + resp_two:
        link.wait_recv()

    front = list(links)

    def push(i):
        grsib_s[i] = gr[quarter(i, 1 - c)].astype(BF)
        return remote(grsib_s.at[i], grsib_r.at[i], SIB)

    def join(i, link):
        link.wait_recv()
        gr[quarter(i, c)] += grsib_r[i].astype(F32)

    def hop(i, to):
        return [
            remote(grsend.at[i, cut(k)], grrecv.at[i, cut(k)], to, False) for k in pieces
        ]

    def fill(i, k):
        grsend[i, cut(k)] = gr[piece(i, c, k)].astype(BF)

    def add(slot, i, k):
        gr[piece(slot, c, k)] += grrecv[i, cut(k)].astype(F32)

    home_pair, home_down, home_up, home_z = hop(2, PAIR), hop(1, DOWN), hop(3, UP), hop(4, BEHIND)

    def send_soon():
        @pl.when(odd == 0)
        def _():
            for k in pieces:
                fill(3, k)
                home_up[k].start()

        @pl.when(odd == 1)
        def _():
            for k in pieces:
                fill(1, k)
                home_down[k].start()

    scale, bias = scale_ref[0], bias_ref[0]
    loss = jnp.zeros((8, ROWS), F32)

    def met(kind, p):
        return pl.ds(pl.multiple_of((2 * p + kind * (1 - l)) * HALF, 64), ROWS)

    soon = 4 - pair_from
    for kind in (1, 0):
        if kind == 0:
            for link in p_opp:
                link.wait_recv()
        for p in (1, 0):
            slots = met(kind, p)

            def column(hh, s):
                at = 4 * p + s
                return vrows[kind, quarter(hh, c), at:at + 1]

            weight = jnp.concatenate(
                [jnp.where(early, column(hh, kind), column(hh, kind + 2)) for hh in (0, 1)], axis=0
            )
            goal = target[kind, p]
            z = scale * dot(emb_p[kind], emb_r[slots], NT) + bias
            e = jnp.exp(-jnp.abs(z))
            soft = jnp.maximum(z, 0.0) + jnp.log1p(e)
            sig = jnp.where(z >= 0, 1.0, e) / (1.0 + e)
            cost = weight * (soft - goal * z)
            loss = loss + jnp.sum(cost.reshape(HALF // 8, 8, ROWS), axis=0)
            coef = (scale * weight * (sig - goal)).astype(BF)
            coefs[kind, p] = coef
            term_r = dot(coef, emb_p[kind], TN)
            if kind == 1:
                gr[slots] = term_r
            else:
                gr[slots] += term_r

    gathers = []

    def gather(value, me, total, peer_of):
        stage = len(gathers)
        lmsg[stage] = value
        lbuf[stage, me] = value
        gathers.append(
            [remote(lmsg.at[stage], lbuf.at[stage, me], peer_of(k)) for k in range(1, total)]
        )

    def gathered(stage, total):
        for copy in gathers[stage]:
            copy.wait_recv()
        return jnp.sum(lbuf[stage, :total], axis=0)

    sib_pair, sib_soon, sib_late, sib_four, sib_zero = [push(i) for i in (2, soon, pair_from, 4, 0)]
    for kind in (0, 1):
        gp[kind] = dot(coefs[kind, 0], emb_r[met(kind, 0)]) + dot(coefs[kind, 1], emb_r[met(kind, 1)])
        if kind == 0:
            gpsend[0] = gp[0, part(1 - h)].astype(BF)
            g_opp = [
                remote(gpsend.at[0, cut(k)], gprecv.at[0, cut(k)], NEAR) for k in pieces
            ]
    join(2, sib_pair)
    for k in pieces:
        fill(2, k)
        home_pair[k].start()
    join(soon, sib_soon)
    send_soon()
    join(pair_from, sib_late)
    lanes = [loss[:, 128 * i:128 * (i + 1)] for i in range(ROWS // 128)]
    gather(lanes[0] + lanes[1] + lanes[2], group_id, 8, group_peer)
    gpsend[1] = gp[1, part(h)].astype(BF)
    join(4, sib_four)
    join(0, sib_zero)
    g_far, g_near = [], []
    for k in pieces:
        g_opp[k].wait_recv()
        at = rows_at((1 - h) * QUART + k * PIECE, PIECE)
        gpsend[2, cut(k)] = (gp[1, at] + gprecv[0, cut(k)].astype(F32)).astype(BF)
        g_far.append(remote(gpsend.at[2, cut(k)], gprecv.at[2, cut(k)], FAR))
        g_near.append(remote(gpsend.at[1, cut(k)], gprecv.at[1, cut(k)], NEAR))
        home_pair[k].wait_recv()
        add(pair_from, 2, k)

        @pl.when(odd == 0)
        def _():
            fill(1, k)
            home_down[k].start()

        @pl.when(odd == 1)
        def _():
            fill(3, k)
            home_up[k].start()

    gather(gathered(0, 8), y, 4, y_peer)
    settle(front)
    middle = [link for link in links if link not in home_z]

    d_far, d_sib, o_near = [[], []], [[], []], [[], []]

    def back(w, k, g):
        u = unit[w, cut(k)]
        inner = jnp.sum(u * g, axis=1, keepdims=True)
        dsend[w, cut(k)] = ((g - u * inner) / norm[w, cut(k), 0:1]).astype(BF)
        d_far[w].append(remote(dsend.at[w, cut(k)], dbuf.at[w, piece(0, c, k)], FAR))

    def product(w, rows):
        d = dsend[w, rows]
        count = rows.stop - rows.start
        for core, to in ((0, NEAR), (1, NEARX)):
            osend[w, core, rows] = dot(d, projs[w, core], NT).astype(BF)
            at = rows_at(c * QUART + rows.start, count)
            o_near[w].append(remote(osend.at[w, core, rows], onear.at[w, at], to))

    def forward(w):
        for k in pieces:
            d_far[w][k].wait_recv()
            at = piece(0, c, k)
            d_sib[w].append(remote(dbuf.at[w, at], dbuf.at[w, at], SIB))

    for k in pieces:
        home_down[k].wait_recv()
        add(up_from, 1, k)
        home_up[k].wait_recv()
        add(down_from, 3, k)
        fill(4, k)
        home_z[k].start()
        g_near[k].wait_recv()
        g_far[k].wait_recv()
        at = rows_at(h * QUART + k * PIECE, PIECE)
        back(1, k, gp[0, at] + gprecv[1, cut(k)].astype(F32) + gprecv[2, cut(k)].astype(F32))
    gather(gathered(1, 4), b // 8, 8, z_peer)
    settle(middle)
    for k in pieces:
        home_z[k].wait_recv()
        back(0, k, gr[piece(0, c, k)] + grrecv[4, cut(k)].astype(F32))
        if k == 0:
            product(1, slice(0, QUART))
        if k == 1:
            product(0, slice(0, 2 * PIECE))
            forward(1)
    product(0, slice(2 * PIECE, QUART))

    def place(w, half, block):
        @pl.when(half == 0)
        def _():
            oval[w, :, :HALF] = block

        @pl.when(half == 1)
        def _():
            oval[w, :, HALF:] = block

    for w in (1, 0):
        if w == 0:
            settle(links)
            forward(0)
        for link in o_near[w]:
            link.wait_recv()
        place(w, h, onear[w].astype(F32).T.astype(BF))
        for link in d_sib[w]:
            link.wait_recv()
        place(w, 1 - h, dot(projs[w, 0], dbuf[w], NT).astype(BF))
    loss_ref[0] = jnp.sum(gathered(2, 8)) / (ROWS * BLOCKS * STEPS * ROWS)
    settle(links)


def deliver(grads, out_r, out_p, sem):
    copies = [pltpu.make_async_copy(grads.at[w], (out_r, out_p)[w], sem.at[w]) for w in (0, 1)]
    for copy in copies:
        copy.start()
    for copy in copies:
        copy.wait()


def on_device(
    prompt_feats, response_feats, prompt_proj, response_proj,
    logit_scale, logit_bias, teacher, valid,
):
    anywhere = pl.BlockSpec(memory_space=pl.ANY)
    scalar = pl.BlockSpec(memory_space=pltpu.SMEM)

    def vm(*shape, kind=BF):
        return pltpu.VMEM(shape, kind)

    grads, loss = pl.pallas_call(
        kernel,
        out_shape=(
            pltpu.VMEM((2, FEAT, ROWS), BF),
            jax.ShapeDtypeStruct((1,), F32),
        ),
        in_specs=[anywhere] * 4 + [scalar] * 2 + [anywhere] * 2,
        out_specs=(pl.BlockSpec(memory_space=pltpu.VMEM), scalar),
        scratch_shapes=[
            vm(2, FEAT, ROWS),
            vm(2, ROWS, FEAT),
            vm(2, 2, FEAT, EMB),
            vm(2, HALF, EMB, kind=F32),
            vm(2, QUART, EMB),
            vm(2, QUART, EMB),
            vm(2, 2, QUART, FEAT),
            vm(2, QUART, EMB),
            vm(2, QUART, EMB),
            vm(2, QUART, EMB, kind=F32),
            vm(2, QUART, 128, kind=F32),
            vm(2, HALF, EMB),
            vm(SLOTS * HALF, EMB),
            vm(2, QUART, STEPS * ROWS, kind=jnp.int32),
            vm(2, HALF, ROWS),
            vm(2, HALF, ROWS),
            vm(2, 2, HALF, ROWS, kind=F32),
            vm(2, STEPS, ROWS, kind=jnp.int32),
            vm(2, ROWS, STEPS, kind=F32),
            vm(2, 2, HALF, ROWS),
            vm(2, HALF, EMB, kind=F32),
            vm(SLOTS * HALF, EMB, kind=F32),
            vm(3, QUART, EMB),
            vm(3, QUART, EMB),
            vm(SLOTS, QUART, EMB),
            vm(SLOTS, QUART, EMB),
            vm(SLOTS, QUART, EMB),
            vm(SLOTS, QUART, EMB),
            vm(2, QUART, EMB),
            vm(2, HALF, EMB),
            vm(2, 2, QUART, FEAT),
            vm(2, HALF, FEAT),
            vm(3, 8, 128, kind=F32),
            vm(3, 8, 8, 128, kind=F32),
            pltpu.SemaphoreType.DMA((128,)),
            pltpu.SemaphoreType.DMA((128,)),
            pltpu.SemaphoreType.DMA((16,)),
        ],
        compiler_params=pltpu.CompilerParams(
            collective_id=0, has_side_effects=True, vmem_limit_bytes=56 * 2**20
        ),
        name="band",
    )(
        response_feats.T, prompt_feats.T, response_proj, prompt_proj,
        logit_scale, logit_bias, teacher, valid.T,
    )
    grad_response, grad_prompt = pl.pallas_call(
        deliver,
        out_shape=(jax.ShapeDtypeStruct((FEAT, ROWS), BF),) * 2,
        in_specs=[pl.BlockSpec(memory_space=pltpu.VMEM)],
        out_specs=(anywhere, anywhere),
        scratch_shapes=[pltpu.SemaphoreType.DMA((2,))],
        name="deliver",
    )(pltpu.with_memory_space_constraint(grads, pltpu.VMEM))
    return grad_prompt.T, grad_response.T, loss


def solution(mesh):
    in_specs = (
        P("batch", "tower"), P("batch", "tower"), P("tower", None), P("tower", None),
        P(), P(), P("batch", None), P("batch", None),
    )
    out_specs = (P("batch", "tower"), P("batch", "tower"), P())
    return jax.shard_map(
        on_device, mesh=mesh, in_specs=in_specs, out_specs=out_specs, check_vma=False
    )
```

```python
import jax
import jax.numpy as jnp
from jax import lax
from jax.experimental import pallas as pl
from jax.experimental.pallas import tpu as pltpu
from jax.sharding import PartitionSpec as P

BF, F32 = jnp.bfloat16, jnp.float32
ROWS, FEAT, EMB, STEPS, BLOCKS, TOWER = 384, 288, 1152, 8, 64, 4
HALF, QUART = ROWS // 2, ROWS // 4
SLOTS, PIECE = 5, 32
NT = (((1,), (1,)), ((), ()))
TN = (((0,), (0,)), ((), ()))


def dot(a, b, dims=(((1,), (0,)), ((), ()))):
    return lax.dot_general(a, b, dims, preferred_element_type=F32)


def sigmoid(x):
    e = jnp.exp(-jnp.abs(x))
    return jnp.where(x >= 0, 1.0, e) / (1.0 + e)


def kernel(
    feats_r, feats_p, proj_r, proj_p, scale_ref, bias_ref, teach, valid,
    oval, loss_ref,
    fcols, frows, projs, part_sum, sib_send, sib_recv, feat_n, fsend, frecv, unit, norm, emb_p, emb_r,
    traw, tsend, trecv, target, vcols, vrows, coefs, gp, gr, gpsend, gprecv,
    grsib_s, grsib_r, grsend, grrecv, dsend, dbuf, osend, onear,
    losses, lmsg, lbuf, send_sem, recv_sem, loc_sem,
):
    b = lax.axis_index("batch")
    t = lax.axis_index("tower")
    l = lax.rem(b, 2)
    h, c = t // 2, lax.rem(t, 2)
    nb = b + 1 - 2 * l
    st = t + 1 - 2 * c
    ft = lax.rem(t + 2, TOWER)
    plane = (b // 8) * 8
    inplane = b - plane
    y = inplane // 2
    odd = lax.rem(y, 2)

    def dev(batch, tower):
        return {"batch": batch, "tower": tower}

    SIB, NEAR, NEARX, FAR = dev(b, st), dev(nb, t), dev(nb, st), dev(nb, ft)
    UP, DOWN = dev(plane + lax.rem(inplane + 2, 8), t), dev(plane + lax.rem(inplane + 6, 8), t)
    PAIR = dev(b + 2 - 4 * odd, t)
    AHEAD, BEHIND = dev(lax.rem(b + 8, BLOCKS), t), dev(lax.rem(b + BLOCKS - 8, BLOCKS), t)
    group_id = l * TOWER + t

    def group_peer(k):
        g = lax.rem(group_id + k, 8)
        return dev(b - l + g // TOWER, lax.rem(g, TOWER))

    def y_peer(k):
        return dev(plane + lax.rem(inplane + 2 * k, 8), t)

    def z_peer(k):
        return dev(lax.rem(b + 8 * k, BLOCKS), t)

    barrier = pltpu.get_barrier_semaphore()
    peers = [group_peer(k) for k in range(1, 8)]
    peers += [y_peer(k) for k in range(1, 4)] + [z_peer(k) for k in range(1, 8)]
    for peer in peers:
        pl.semaphore_signal(barrier, inc=1, device_id=peer, device_id_type=pl.DeviceIdType.MESH)

    def rows_at(start, count):
        return pl.ds(pl.multiple_of(start, 16), count)

    def quarter(half, core):
        return rows_at(half * HALF + core * QUART, QUART)

    def part(core):
        return rows_at(core * QUART, QUART)

    def piece(slot, core, k):
        return rows_at(slot * HALF + core * QUART + k * PIECE, PIECE)

    def cut(k):
        return slice(k * PIECE, (k + 1) * PIECE)

    feats, proj = (feats_r, feats_p), (proj_r, proj_p)
    local = []

    def load(src, dst):
        copy = pltpu.make_async_copy(src, dst, loc_sem.at[len(local)])
        copy.start()
        local.append(copy)
        return copy

    links = []

    class Link:
        def __init__(self, copy):
            self.copy, self.waited, self.sent = copy, False, False

        def start(self):
            self.copy.start()

        def wait_recv(self):
            self.waited = True
            self.copy.wait_recv()

    def remote(src, dst, to, start=True):
        k = len(links)
        link = Link(
            pltpu.make_async_remote_copy(
                src_ref=src, dst_ref=dst, send_sem=send_sem.at[k], recv_sem=recv_sem.at[k],
                device_id=to, device_id_type=pl.DeviceIdType.MESH,
            )
        )
        if start:
            link.start()
        links.append(link)
        return link

    def settle(some):
        for link in some:
            if not link.sent:
                link.sent = True
                link.copy.wait_send()

    own_feat = [load(feats[w], fcols.at[w]) for w in (0, 1)]
    own_proj = [load(proj[w], projs.at[w, 0]) for w in (0, 1)]
    own_teach = [load(teach.at[quarter(hh, c)], traw.at[hh]) for hh in (0, 1)]
    own_valid = load(valid, vcols.at[1])

    def own_sum(w):
        own_proj[w].wait()
        part_sum[w] = dot(frows[w, rows_at((1 - h) * HALF, HALF)], projs[w, 0])
        sib_send[w] = part_sum[w, part(1 - c)].astype(BF)

    for w in (0, 1):
        own_feat[w].wait()
        frows[w] = fcols[w].astype(F32).T.astype(BF)
        if w == 0:
            own_sum(0)
    pl.semaphore_wait(barrier, len(peers))

    sum_sib, to_sib, feat_near, feat_nearx, partial = [], [], [], [], []

    def enter(w):
        sum_sib.append(remote(sib_send.at[w], sib_recv.at[w], SIB))
        feat_near.append(remote(frows.at[w, quarter(h, c)], feat_n.at[w, 0], NEAR))
        feat_nearx.append(remote(frows.at[w, quarter(h, 1 - c)], feat_n.at[w, 1], NEARX))

    enter(0)
    own_sum(1)
    enter(1)
    pieces = range(QUART // PIECE)
    for w in (0, 1):
        sum_sib[w].wait_recv()
        fsend[w] = (part_sum[w, part(c)] + sib_recv[w].astype(F32)).astype(BF)
        partial.append(
            [remote(fsend.at[w, cut(k)], frecv.at[w, cut(k)], FAR, w == 0) for k in pieces]
        )
        to_sib.append(remote(proj[w], projs.at[w, 1], SIB))

    for copy in own_teach:
        copy.wait()
    early = lax.broadcasted_iota(jnp.int32, (1, ROWS), 1) < HALF

    def steps_of(hh, s):
        a = traw[hh, :, s * ROWS:(s + 1) * ROWS].astype(F32)
        d = traw[hh, :, (s + 2) * ROWS:(s + 3) * ROWS].astype(F32)
        keep = jnp.where(h == 0, a, d)
        turn = pltpu.roll(jnp.where(h == 0, d, a), HALF, 1)
        lanes = lax.broadcasted_iota(jnp.int32, (QUART, ROWS), 1)
        return jnp.where((lanes < HALF) == (h == 0), keep, turn)

    for p in (0, 1):
        for hh in (0, 1):
            tsend[p, hh * QUART:(hh + 1) * QUART] = steps_of(hh, 4 * p).astype(BF)
    teach_near = remote(tsend, trecv, NEAR)
    valid_near = remote(valid, vcols.at[0], NEAR)
    for p in (0, 1):
        for hh in (0, 1):
            target[1, p, hh * QUART:(hh + 1) * QUART] = sigmoid(steps_of(hh, 4 * p + 1) / 32.0)
    for i in (0, 4):
        gr[i * HALF:(i + 1) * HALF] = jnp.zeros((HALF, EMB), F32)

    def near_sum(w):
        to_sib[w].wait_recv()
        feat_near[w].wait_recv()
        feat_nearx[w].wait_recv()
        unit[w] = dot(feat_n[w, 0], projs[w, 0]) + dot(feat_n[w, 1], projs[w, 1])

    def finish(w, k):
        pre = unit[w, cut(k)] + frecv[w, cut(k)].astype(F32)
        length = jnp.sqrt(jnp.sum(pre * pre, axis=1, keepdims=True) + 1e-06)
        norm[w, cut(k)] = jnp.broadcast_to(length, (PIECE, 128))
        u = pre / length
        unit[w, cut(k)] = u
        return u.astype(BF)

    up_from, down_from, pair_from = (y // 3) * 4, ((y + 3) // 4) * 4, 1 + 2 * odd

    def relay(src, dst, to):
        return [
            remote(emb_r.at[piece(src, c, k)], emb_r.at[piece(dst, c, k)], to, False)
            for k in pieces
        ]

    def resp_over(slot):
        at = quarter(slot, c)
        return remote(emb_r.at[at], emb_r.at[at], SIB)

    zhop = relay(0, 4, AHEAD)
    up, down = relay(up_from, 1, UP), relay(down_from, 3, DOWN)
    pair = relay(pair_from, 2, PAIR)
    near_sum(0)
    for k in pieces:
        partial[0][k].wait_recv()
        partial[1][k].start()
        emb_r[piece(0, c, k)] = finish(0, k)
        zhop[k].start()

        @pl.when(y < 3)
        def _():
            up[k].start()

        @pl.when(y == 0)
        def _():
            down[k].start()

    resp_sib = [None] * SLOTS
    resp_sib[0] = resp_over(0)

    def zrelay(k):
        zhop[k].wait_recv()

        @pl.when(y == 3)
        def _():
            up[k].start()

        @pl.when(y > 0)
        def _():
            down[k].start()

    near_sum(1)
    p_far, p_near, p_opp = [], [], []
    for k in pieces:
        zrelay(k)
        partial[1][k].wait_recv()
        at = rows_at(h * QUART + k * PIECE, PIECE)
        emb_p[0, at] = finish(1, k)
        p_far.append(remote(emb_p.at[0, at], emb_p.at[1, at], FAR))
        p_near.append(remote(emb_p.at[0, at], emb_p.at[1, at], NEAR))
    resp_sib[4] = resp_over(4)

    teach_near.wait_recv()
    for p in (0, 1):
        target[0, p] = sigmoid(trecv[p].astype(F32) / 32.0)
    own_valid.wait()
    valid_near.wait_recv()
    for kind in (0, 1):
        vrows[kind] = vcols[kind].astype(F32).T

    for k in pieces:
        @pl.when(odd == 0)
        def _():
            up[k].wait_recv()

        @pl.when(odd == 1)
        def _():
            down[k].wait_recv()

        pair[k].start()
        p_far[k].wait_recv()
        at = rows_at((1 - h) * QUART + k * PIECE, PIECE)
        p_opp.append(remote(emb_p.at[1, at], emb_p.at[0, at], NEAR))

    for k in pieces:
        @pl.when(odd == 1)
        def _():
            up[k].wait_recv()

        @pl.when(odd == 0)
        def _():
            down[k].wait_recv()

    resp_sib[3], resp_sib[1] = resp_over(3), resp_over(1)
    resp_two = []
    for k in pieces:
        pair[k].wait_recv()
        at = piece(2, c, k)
        resp_two.append(remote(emb_r.at[at], emb_r.at[at], SIB))
    for k in pieces:
        p_near[k].wait_recv()
    for link in [resp_sib[i] for i in (4, 3, 1, 0)]:
        link.wait_recv()

    front = list(links)

    def push(i):
        grsib_s[i] = gr[quarter(i, 1 - c)].astype(BF)
        return remote(grsib_s.at[i], grsib_r.at[i], SIB)

    def join(i, link):
        link.wait_recv()
        gr[quarter(i, c)] += grsib_r[i].astype(F32)

    def hop(i, to):
        return [
            remote(grsend.at[i, cut(k)], grrecv.at[i, cut(k)], to, False) for k in pieces
        ]

    def fill(i, k):
        grsend[i, cut(k)] = gr[piece(i, c, k)].astype(BF)

    def add(slot, i, k):
        gr[piece(slot, c, k)] += grrecv[i, cut(k)].astype(F32)

    home_pair, home_down, home_up, home_z = hop(2, PAIR), hop(1, DOWN), hop(3, UP), hop(4, BEHIND)

    def send_soon():
        @pl.when(odd == 0)
        def _():
            for k in pieces:
                fill(3, k)
                home_up[k].start()

        @pl.when(odd == 1)
        def _():
            for k in pieces:
                fill(1, k)
                home_down[k].start()

    scale, bias = scale_ref[0], bias_ref[0]
    losses[...] = jnp.zeros((8, ROWS), F32)

    def met(kind, p):
        return pl.ds(pl.multiple_of((2 * p + kind * (1 - l)) * HALF, 64), ROWS)

    soon = 4 - pair_from
    def tile(kind, p):
        slots = met(kind, p)

        def column(hh, s):
            at = 4 * p + s
            return vrows[kind, quarter(hh, c), at:at + 1]

        weight = jnp.concatenate(
            [jnp.where(early, column(hh, kind), column(hh, kind + 2)) for hh in (0, 1)], axis=0
        )
        goal = target[kind, p]
        z = scale * dot(emb_p[kind], emb_r[slots], NT) + bias
        e = jnp.exp(-jnp.abs(z))
        soft = jnp.maximum(z, 0.0) + jnp.log1p(e)
        sig = jnp.where(z >= 0, 1.0, e) / (1.0 + e)
        cost = weight * (soft - goal * z)
        losses[...] += jnp.sum(cost.reshape(HALF // 8, 8, ROWS), axis=0)
        coef = (scale * weight * (sig - goal)).astype(BF)
        coefs[kind, p] = coef
        term_r = dot(coef, emb_p[kind], TN)
        if kind == 1:
            gr[slots] = term_r
        else:
            gr[slots] += term_r

    for early_l in (0, 1):
        @pl.when(l == early_l)
        def _():
            tile(1, 1 - early_l)

    for link in resp_two:
        link.wait_recv()
    for early_l in (0, 1):
        @pl.when(l == early_l)
        def _():
            tile(1, early_l)

    for link in p_opp:
        link.wait_recv()
    tile(0, 1)
    tile(0, 0)
    loss = losses[...]

    gathers = []

    def gather(value, me, total, peer_of):
        stage = len(gathers)
        lmsg[stage] = value
        lbuf[stage, me] = value
        gathers.append(
            [remote(lmsg.at[stage], lbuf.at[stage, me], peer_of(k)) for k in range(1, total)]
        )

    def gathered(stage, total):
        for copy in gathers[stage]:
            copy.wait_recv()
        return jnp.sum(lbuf[stage, :total], axis=0)

    sib_pair, sib_soon, sib_late, sib_four, sib_zero = [push(i) for i in (2, soon, pair_from, 4, 0)]
    for kind in (0, 1):
        gp[kind] = dot(coefs[kind, 0], emb_r[met(kind, 0)]) + dot(coefs[kind, 1], emb_r[met(kind, 1)])
        if kind == 0:
            gpsend[0] = gp[0, part(1 - h)].astype(BF)
            g_opp = [
                remote(gpsend.at[0, cut(k)], gprecv.at[0, cut(k)], NEAR) for k in pieces
            ]
    join(2, sib_pair)
    for k in pieces:
        fill(2, k)
        home_pair[k].start()
    join(soon, sib_soon)
    send_soon()
    join(pair_from, sib_late)
    lanes = [loss[:, 128 * i:128 * (i + 1)] for i in range(ROWS // 128)]
    gather(lanes[0] + lanes[1] + lanes[2], group_id, 8, group_peer)
    gpsend[1] = gp[1, part(h)].astype(BF)
    join(4, sib_four)
    join(0, sib_zero)
    g_far, g_near = [], []
    for k in pieces:
        g_opp[k].wait_recv()
        at = rows_at((1 - h) * QUART + k * PIECE, PIECE)
        gpsend[2, cut(k)] = (gp[1, at] + gprecv[0, cut(k)].astype(F32)).astype(BF)
        g_far.append(remote(gpsend.at[2, cut(k)], gprecv.at[2, cut(k)], FAR))
        g_near.append(remote(gpsend.at[1, cut(k)], gprecv.at[1, cut(k)], NEAR))
        home_pair[k].wait_recv()
        add(pair_from, 2, k)

        @pl.when(odd == 0)
        def _():
            fill(1, k)
            home_down[k].start()

        @pl.when(odd == 1)
        def _():
            fill(3, k)
            home_up[k].start()

    gather(gathered(0, 8), y, 4, y_peer)
    settle(front)
    middle = [link for link in links if link not in home_z]

    d_far, d_sib, o_near = [[], []], [[], []], [[], []]

    def back(w, k, g):
        u = unit[w, cut(k)]
        inner = jnp.sum(u * g, axis=1, keepdims=True)
        dsend[w, cut(k)] = ((g - u * inner) / norm[w, cut(k), 0:1]).astype(BF)
        d_far[w].append(remote(dsend.at[w, cut(k)], dbuf.at[w, piece(0, c, k)], FAR))

    def product(w, rows):
        d = dsend[w, rows]
        count = rows.stop - rows.start
        for core, to in ((0, NEAR), (1, NEARX)):
            osend[w, core, rows] = dot(d, projs[w, core], NT).astype(BF)
            at = rows_at(c * QUART + rows.start, count)
            o_near[w].append(remote(osend.at[w, core, rows], onear.at[w, at], to))

    def forward(w):
        for k in pieces:
            d_far[w][k].wait_recv()
            at = piece(0, c, k)
            d_sib[w].append(remote(dbuf.at[w, at], dbuf.at[w, at], SIB))

    for k in pieces:
        home_down[k].wait_recv()
        add(up_from, 1, k)
        home_up[k].wait_recv()
        add(down_from, 3, k)
        fill(4, k)
        home_z[k].start()
        g_near[k].wait_recv()
        g_far[k].wait_recv()
        at = rows_at(h * QUART + k * PIECE, PIECE)
        back(1, k, gp[0, at] + gprecv[1, cut(k)].astype(F32) + gprecv[2, cut(k)].astype(F32))
    gather(gathered(1, 4), b // 8, 8, z_peer)
    settle(middle)
    for k in pieces:
        home_z[k].wait_recv()
        back(0, k, gr[piece(0, c, k)] + grrecv[4, cut(k)].astype(F32))
        if k == 0:
            product(1, slice(0, QUART))
        if k == 1:
            product(0, slice(0, 2 * PIECE))
            forward(1)
    product(0, slice(2 * PIECE, QUART))

    def place(w, half, block):
        @pl.when(half == 0)
        def _():
            oval[w, :, :HALF] = block

        @pl.when(half == 1)
        def _():
            oval[w, :, HALF:] = block

    for w in (1, 0):
        if w == 0:
            settle(links)
            forward(0)
        for link in o_near[w]:
            link.wait_recv()
        place(w, h, onear[w].astype(F32).T.astype(BF))
        for link in d_sib[w]:
            link.wait_recv()
        place(w, 1 - h, dot(projs[w, 0], dbuf[w], NT).astype(BF))
    loss_ref[0] = jnp.sum(gathered(2, 8)) / (ROWS * BLOCKS * STEPS * ROWS)
    settle(links)


def deliver(grads, out_r, out_p, sem):
    copies = [pltpu.make_async_copy(grads.at[w], (out_r, out_p)[w], sem.at[w]) for w in (0, 1)]
    for copy in copies:
        copy.start()
    for copy in copies:
        copy.wait()


def on_device(
    prompt_feats, response_feats, prompt_proj, response_proj,
    logit_scale, logit_bias, teacher, valid,
):
    anywhere = pl.BlockSpec(memory_space=pl.ANY)
    scalar = pl.BlockSpec(memory_space=pltpu.SMEM)

    def vm(*shape, kind=BF):
        return pltpu.VMEM(shape, kind)

    grads, loss = pl.pallas_call(
        kernel,
        out_shape=(
            pltpu.VMEM((2, FEAT, ROWS), BF),
            jax.ShapeDtypeStruct((1,), F32),
        ),
        in_specs=[anywhere] * 4 + [scalar] * 2 + [anywhere] * 2,
        out_specs=(pl.BlockSpec(memory_space=pltpu.VMEM), scalar),
        scratch_shapes=[
            vm(2, FEAT, ROWS),
            vm(2, ROWS, FEAT),
            vm(2, 2, FEAT, EMB),
            vm(2, HALF, EMB, kind=F32),
            vm(2, QUART, EMB),
            vm(2, QUART, EMB),
            vm(2, 2, QUART, FEAT),
            vm(2, QUART, EMB),
            vm(2, QUART, EMB),
            vm(2, QUART, EMB, kind=F32),
            vm(2, QUART, 128, kind=F32),
            vm(2, HALF, EMB),
            vm(SLOTS * HALF, EMB),
            vm(2, QUART, STEPS * ROWS, kind=jnp.int32),
            vm(2, HALF, ROWS),
            vm(2, HALF, ROWS),
            vm(2, 2, HALF, ROWS, kind=F32),
            vm(2, STEPS, ROWS, kind=jnp.int32),
            vm(2, ROWS, STEPS, kind=F32),
            vm(2, 2, HALF, ROWS),
            vm(2, HALF, EMB, kind=F32),
            vm(SLOTS * HALF, EMB, kind=F32),
            vm(3, QUART, EMB),
            vm(3, QUART, EMB),
            vm(SLOTS, QUART, EMB),
            vm(SLOTS, QUART, EMB),
            vm(SLOTS, QUART, EMB),
            vm(SLOTS, QUART, EMB),
            vm(2, QUART, EMB),
            vm(2, HALF, EMB),
            vm(2, 2, QUART, FEAT),
            vm(2, HALF, FEAT),
            vm(8, ROWS, kind=F32),
            vm(3, 8, 128, kind=F32),
            vm(3, 8, 8, 128, kind=F32),
            pltpu.SemaphoreType.DMA((128,)),
            pltpu.SemaphoreType.DMA((128,)),
            pltpu.SemaphoreType.DMA((16,)),
        ],
        compiler_params=pltpu.CompilerParams(
            collective_id=0, has_side_effects=True, vmem_limit_bytes=56 * 2**20
        ),
        name="band",
    )(
        response_feats.T, prompt_feats.T, response_proj, prompt_proj,
        logit_scale, logit_bias, teacher, valid.T,
    )
    grad_response, grad_prompt = pl.pallas_call(
        deliver,
        out_shape=(jax.ShapeDtypeStruct((FEAT, ROWS), BF),) * 2,
        in_specs=[pl.BlockSpec(memory_space=pltpu.VMEM)],
        out_specs=(anywhere, anywhere),
        scratch_shapes=[pltpu.SemaphoreType.DMA((2,))],
        name="deliver",
    )(pltpu.with_memory_space_constraint(grads, pltpu.VMEM))
    return grad_prompt.T, grad_response.T, loss


def solution(mesh):
    in_specs = (
        P("batch", "tower"), P("batch", "tower"), P("tower", None), P("tower", None),
        P(), P(), P("batch", None), P("batch", None),
    )
    out_specs = (P("batch", "tower"), P("batch", "tower"), P())
    return jax.shard_map(
        on_device, mesh=mesh, in_specs=in_specs, out_specs=out_specs, check_vma=False
    )
```

```python
import jax
import jax.numpy as jnp
from jax import lax
from jax.experimental import pallas as pl
from jax.experimental.pallas import tpu as pltpu
from jax.sharding import PartitionSpec as P

BF, F32 = jnp.bfloat16, jnp.float32
ROWS, FEAT, EMB, STEPS, BLOCKS, TOWER = 384, 288, 1152, 8, 64, 4
HALF, QUART = ROWS // 2, ROWS // 4
SLOTS, PIECE = 5, 32
NT = (((1,), (1,)), ((), ()))
TN = (((0,), (0,)), ((), ()))


def dot(a, b, dims=(((1,), (0,)), ((), ()))):
    return lax.dot_general(a, b, dims, preferred_element_type=F32)


def sigmoid(x):
    e = jnp.exp(-jnp.abs(x))
    return jnp.where(x >= 0, 1.0, e) / (1.0 + e)


def kernel(
    feats_r, feats_p, proj_r, proj_p, scale_ref, bias_ref, teach, valid,
    oval, loss_ref,
    fcols, frows, projs, part_sum, sib_send, sib_recv, feat_n, fsend, frecv, unit, norm, emb_p, emb_r,
    traw, tsend, trecv, target, vcols, vrows, coefs, gp, gr, gpsend, gprecv,
    grsib_s, grsib_r, grsend, grrecv, dsend, dbuf, osend, onear,
    losses, lmsg, lbuf, send_sem, recv_sem, loc_sem,
):
    b = lax.axis_index("batch")
    t = lax.axis_index("tower")
    l = lax.rem(b, 2)
    h, c = t // 2, lax.rem(t, 2)
    nb = b + 1 - 2 * l
    st = t + 1 - 2 * c
    ft = lax.rem(t + 2, TOWER)
    plane = (b // 8) * 8
    inplane = b - plane
    y = inplane // 2
    odd = lax.rem(y, 2)

    def dev(batch, tower):
        return {"batch": batch, "tower": tower}

    SIB, NEAR, NEARX, FAR = dev(b, st), dev(nb, t), dev(nb, st), dev(nb, ft)
    UP, DOWN = dev(plane + lax.rem(inplane + 2, 8), t), dev(plane + lax.rem(inplane + 6, 8), t)
    PAIR = dev(b + 2 - 4 * odd, t)
    AHEAD, BEHIND = dev(lax.rem(b + 8, BLOCKS), t), dev(lax.rem(b + BLOCKS - 8, BLOCKS), t)
    group_id = l * TOWER + t

    def group_peer(k):
        g = lax.rem(group_id + k, 8)
        return dev(b - l + g // TOWER, lax.rem(g, TOWER))

    def y_peer(k):
        return dev(plane + lax.rem(inplane + 2 * k, 8), t)

    def z_peer(k):
        return dev(lax.rem(b + 8 * k, BLOCKS), t)

    barrier = pltpu.get_barrier_semaphore()
    peers = [group_peer(k) for k in range(1, 8)]
    peers += [y_peer(k) for k in range(1, 4)] + [z_peer(k) for k in range(1, 8)]
    for peer in peers:
        pl.semaphore_signal(barrier, inc=1, device_id=peer, device_id_type=pl.DeviceIdType.MESH)

    def rows_at(start, count):
        return pl.ds(pl.multiple_of(start, 16), count)

    def quarter(half, core):
        return rows_at(half * HALF + core * QUART, QUART)

    def part(core):
        return rows_at(core * QUART, QUART)

    def piece(slot, core, k):
        return rows_at(slot * HALF + core * QUART + k * PIECE, PIECE)

    def cut(k):
        return slice(k * PIECE, (k + 1) * PIECE)

    feats, proj = (feats_r, feats_p), (proj_r, proj_p)
    local = []

    def load(src, dst):
        copy = pltpu.make_async_copy(src, dst, loc_sem.at[len(local)])
        copy.start()
        local.append(copy)
        return copy

    links = []

    class Link:
        def __init__(self, copy):
            self.copy, self.waited, self.sent = copy, False, False

        def start(self):
            self.copy.start()

        def wait_recv(self):
            self.waited = True
            self.copy.wait_recv()

    def remote(src, dst, to, start=True):
        k = len(links)
        link = Link(
            pltpu.make_async_remote_copy(
                src_ref=src, dst_ref=dst, send_sem=send_sem.at[k], recv_sem=recv_sem.at[k],
                device_id=to, device_id_type=pl.DeviceIdType.MESH,
            )
        )
        if start:
            link.start()
        links.append(link)
        return link

    def settle(some):
        for link in some:
            if not link.sent:
                link.sent = True
                link.copy.wait_send()

    own_feat = [load(feats[w], fcols.at[w]) for w in (0, 1)]
    own_proj = [load(proj[w], projs.at[w, 0]) for w in (0, 1)]
    own_teach = [load(teach.at[quarter(hh, c)], traw.at[hh]) for hh in (0, 1)]
    own_valid = load(valid, vcols.at[1])

    def own_sum(w):
        own_proj[w].wait()
        part_sum[w] = dot(frows[w, rows_at((1 - h) * HALF, HALF)], projs[w, 0])
        sib_send[w] = part_sum[w, part(1 - c)].astype(BF)

    def turn(w):
        own_feat[w].wait()
        frows[w] = fcols[w].astype(F32).T.astype(BF)

    turn(0)
    own_sum(0)
    pl.semaphore_wait(barrier, len(peers))

    sum_sib, to_sib, feat_near, feat_nearx, partial = [], [], [], [], []

    def enter(w):
        sum_sib.append(remote(sib_send.at[w], sib_recv.at[w], SIB))
        feat_near.append(remote(frows.at[w, quarter(h, c)], feat_n.at[w, 0], NEAR))
        feat_nearx.append(remote(frows.at[w, quarter(h, 1 - c)], feat_n.at[w, 1], NEARX))

    enter(0)
    turn(1)
    own_sum(1)
    enter(1)
    pieces = range(QUART // PIECE)
    for w in (0, 1):
        sum_sib[w].wait_recv()
        fsend[w] = (part_sum[w, part(c)] + sib_recv[w].astype(F32)).astype(BF)
        partial.append(
            [remote(fsend.at[w, cut(k)], frecv.at[w, cut(k)], FAR, w == 0) for k in pieces]
        )
        to_sib.append(remote(proj[w], projs.at[w, 1], SIB))

    for copy in own_teach:
        copy.wait()
    early = lax.broadcasted_iota(jnp.int32, (1, ROWS), 1) < HALF

    def steps_of(hh, s):
        a = traw[hh, :, s * ROWS:(s + 1) * ROWS].astype(F32)
        d = traw[hh, :, (s + 2) * ROWS:(s + 3) * ROWS].astype(F32)
        keep = jnp.where(h == 0, a, d)
        turn = pltpu.roll(jnp.where(h == 0, d, a), HALF, 1)
        lanes = lax.broadcasted_iota(jnp.int32, (QUART, ROWS), 1)
        return jnp.where((lanes < HALF) == (h == 0), keep, turn)

    for p in (0, 1):
        for hh in (0, 1):
            tsend[p, hh * QUART:(hh + 1) * QUART] = steps_of(hh, 4 * p).astype(BF)
    teach_near = remote(tsend, trecv, NEAR)
    valid_near = remote(valid, vcols.at[0], NEAR)
    for p in (0, 1):
        for hh in (0, 1):
            target[1, p, hh * QUART:(hh + 1) * QUART] = sigmoid(steps_of(hh, 4 * p + 1) / 32.0)
    for i in (0, 4):
        gr[i * HALF:(i + 1) * HALF] = jnp.zeros((HALF, EMB), F32)

    def near_sum(w):
        to_sib[w].wait_recv()
        feat_near[w].wait_recv()
        feat_nearx[w].wait_recv()
        unit[w] = dot(feat_n[w, 0], projs[w, 0]) + dot(feat_n[w, 1], projs[w, 1])

    def finish(w, k):
        pre = unit[w, cut(k)] + frecv[w, cut(k)].astype(F32)
        length = jnp.sqrt(jnp.sum(pre * pre, axis=1, keepdims=True) + 1e-06)
        norm[w, cut(k)] = jnp.broadcast_to(length, (PIECE, 128))
        u = pre / length
        unit[w, cut(k)] = u
        return u.astype(BF)

    up_from, down_from, pair_from = (y // 3) * 4, ((y + 3) // 4) * 4, 1 + 2 * odd

    def relay(src, dst, to):
        return [
            remote(emb_r.at[piece(src, c, k)], emb_r.at[piece(dst, c, k)], to, False)
            for k in pieces
        ]

    def resp_over(slot):
        at = quarter(slot, c)
        return remote(emb_r.at[at], emb_r.at[at], SIB)

    zhop = relay(0, 4, AHEAD)
    up, down = relay(up_from, 1, UP), relay(down_from, 3, DOWN)
    pair = relay(pair_from, 2, PAIR)
    near_sum(0)
    for k in pieces:
        partial[0][k].wait_recv()
        partial[1][k].start()
        emb_r[piece(0, c, k)] = finish(0, k)
        zhop[k].start()

        @pl.when(y < 3)
        def _():
            up[k].start()

        @pl.when(y == 0)
        def _():
            down[k].start()

    resp_sib = [None] * SLOTS
    resp_sib[0] = resp_over(0)

    def zrelay(k):
        zhop[k].wait_recv()

        @pl.when(y == 3)
        def _():
            up[k].start()

        @pl.when(y > 0)
        def _():
            down[k].start()

    near_sum(1)
    p_far, p_near, p_opp = [], [], []
    for k in pieces:
        zrelay(k)
        partial[1][k].wait_recv()
        at = rows_at(h * QUART + k * PIECE, PIECE)
        emb_p[0, at] = finish(1, k)
        p_far.append(remote(emb_p.at[0, at], emb_p.at[1, at], FAR))
        p_near.append(remote(emb_p.at[0, at], emb_p.at[1, at], NEAR))
    resp_sib[4] = resp_over(4)

    teach_near.wait_recv()
    for p in (0, 1):
        target[0, p] = sigmoid(trecv[p].astype(F32) / 32.0)
    own_valid.wait()
    valid_near.wait_recv()
    for kind in (0, 1):
        vrows[kind] = vcols[kind].astype(F32).T

    for k in pieces:
        @pl.when(odd == 0)
        def _():
            up[k].wait_recv()

        @pl.when(odd == 1)
        def _():
            down[k].wait_recv()

        pair[k].start()
        p_far[k].wait_recv()
        at = rows_at((1 - h) * QUART + k * PIECE, PIECE)
        p_opp.append(remote(emb_p.at[1, at], emb_p.at[0, at], NEAR))

    for k in pieces:
        @pl.when(odd == 1)
        def _():
            up[k].wait_recv()

        @pl.when(odd == 0)
        def _():
            down[k].wait_recv()

    resp_sib[3], resp_sib[1] = resp_over(3), resp_over(1)
    resp_two = []
    for k in pieces:
        pair[k].wait_recv()
        at = piece(2, c, k)
        resp_two.append(remote(emb_r.at[at], emb_r.at[at], SIB))
    for k in pieces:
        p_near[k].wait_recv()
    for link in [resp_sib[i] for i in (4, 3, 1, 0)]:
        link.wait_recv()

    front = list(links)

    def push(i):
        grsib_s[i] = gr[quarter(i, 1 - c)].astype(BF)
        return remote(grsib_s.at[i], grsib_r.at[i], SIB)

    def join(i, link):
        link.wait_recv()
        gr[quarter(i, c)] += grsib_r[i].astype(F32)

    def hop(i, to):
        return [
            remote(grsend.at[i, cut(k)], grrecv.at[i, cut(k)], to, False) for k in pieces
        ]

    def fill(i, k):
        grsend[i, cut(k)] = gr[piece(i, c, k)].astype(BF)

    def add(slot, i, k):
        gr[piece(slot, c, k)] += grrecv[i, cut(k)].astype(F32)

    home_pair, home_down, home_up, home_z = hop(2, PAIR), hop(1, DOWN), hop(3, UP), hop(4, BEHIND)

    def send_soon():
        @pl.when(odd == 0)
        def _():
            for k in pieces:
                fill(3, k)
                home_up[k].start()

        @pl.when(odd == 1)
        def _():
            for k in pieces:
                fill(1, k)
                home_down[k].start()

    scale, bias = scale_ref[0], bias_ref[0]
    losses[...] = jnp.zeros((8, ROWS), F32)

    def met(kind, p):
        return pl.ds(pl.multiple_of((2 * p + kind * (1 - l)) * HALF, 64), ROWS)

    soon = 4 - pair_from
    def tile(kind, p):
        slots = met(kind, p)

        def column(hh, s):
            at = 4 * p + s
            return vrows[kind, quarter(hh, c), at:at + 1]

        weight = jnp.concatenate(
            [jnp.where(early, column(hh, kind), column(hh, kind + 2)) for hh in (0, 1)], axis=0
        )
        goal = target[kind, p]
        z = scale * dot(emb_p[kind], emb_r[slots], NT) + bias
        e = jnp.exp(-jnp.abs(z))
        soft = jnp.maximum(z, 0.0) + jnp.log1p(e)
        sig = jnp.where(z >= 0, 1.0, e) / (1.0 + e)
        cost = weight * (soft - goal * z)
        losses[...] += jnp.sum(cost.reshape(HALF // 8, 8, ROWS), axis=0)
        coef = (scale * weight * (sig - goal)).astype(BF)
        coefs[kind, p] = coef
        term_r = dot(coef, emb_p[kind], TN)
        if kind == 1:
            gr[slots] = term_r
        else:
            gr[slots] += term_r

    for early_l in (0, 1):
        @pl.when(l == early_l)
        def _():
            tile(1, 1 - early_l)

    for link in resp_two:
        link.wait_recv()
    for early_l in (0, 1):
        @pl.when(l == early_l)
        def _():
            tile(1, early_l)

    for link in p_opp:
        link.wait_recv()
    tile(0, 1)
    tile(0, 0)
    loss = losses[...]

    gathers = []

    def gather(value, me, total, peer_of):
        stage = len(gathers)
        lmsg[stage] = value
        lbuf[stage, me] = value
        gathers.append(
            [remote(lmsg.at[stage], lbuf.at[stage, me], peer_of(k)) for k in range(1, total)]
        )

    def gathered(stage, total):
        for copy in gathers[stage]:
            copy.wait_recv()
        return jnp.sum(lbuf[stage, :total], axis=0)

    sib_pair, sib_soon, sib_late, sib_four, sib_zero = [push(i) for i in (2, soon, pair_from, 4, 0)]
    for kind in (0, 1):
        gp[kind] = dot(coefs[kind, 0], emb_r[met(kind, 0)]) + dot(coefs[kind, 1], emb_r[met(kind, 1)])
        if kind == 0:
            gpsend[0] = gp[0, part(1 - h)].astype(BF)
            g_opp = [
                remote(gpsend.at[0, cut(k)], gprecv.at[0, cut(k)], NEAR) for k in pieces
            ]
    join(2, sib_pair)
    for k in pieces:
        fill(2, k)
        home_pair[k].start()
    join(soon, sib_soon)
    send_soon()
    join(pair_from, sib_late)
    lanes = [loss[:, 128 * i:128 * (i + 1)] for i in range(ROWS // 128)]
    gather(lanes[0] + lanes[1] + lanes[2], group_id, 8, group_peer)
    gpsend[1] = gp[1, part(h)].astype(BF)
    join(4, sib_four)
    join(0, sib_zero)
    g_far, g_near = [], []
    for k in pieces:
        g_opp[k].wait_recv()
        at = rows_at((1 - h) * QUART + k * PIECE, PIECE)
        gpsend[2, cut(k)] = (gp[1, at] + gprecv[0, cut(k)].astype(F32)).astype(BF)
        g_far.append(remote(gpsend.at[2, cut(k)], gprecv.at[2, cut(k)], FAR))
        g_near.append(remote(gpsend.at[1, cut(k)], gprecv.at[1, cut(k)], NEAR))
        home_pair[k].wait_recv()
        add(pair_from, 2, k)

        @pl.when(odd == 0)
        def _():
            fill(1, k)
            home_down[k].start()

        @pl.when(odd == 1)
        def _():
            fill(3, k)
            home_up[k].start()

    gather(gathered(0, 8), y, 4, y_peer)
    settle(front)
    middle = [link for link in links if link not in home_z]

    d_far, d_sib, o_near = [[], []], [[], []], [[], []]

    def back(w, k, g):
        u = unit[w, cut(k)]
        inner = jnp.sum(u * g, axis=1, keepdims=True)
        dsend[w, cut(k)] = ((g - u * inner) / norm[w, cut(k), 0:1]).astype(BF)
        d_far[w].append(remote(dsend.at[w, cut(k)], dbuf.at[w, piece(0, c, k)], FAR))

    def product(w, rows):
        d = dsend[w, rows]
        count = rows.stop - rows.start
        for core, to in ((0, NEAR), (1, NEARX)):
            osend[w, core, rows] = dot(d, projs[w, core], NT).astype(BF)
            at = rows_at(c * QUART + rows.start, count)
            o_near[w].append(remote(osend.at[w, core, rows], onear.at[w, at], to))

    def forward(w):
        for k in pieces:
            d_far[w][k].wait_recv()
            at = piece(0, c, k)
            d_sib[w].append(remote(dbuf.at[w, at], dbuf.at[w, at], SIB))

    for k in pieces:
        home_down[k].wait_recv()
        add(up_from, 1, k)
        home_up[k].wait_recv()
        add(down_from, 3, k)
        fill(4, k)
        home_z[k].start()
        g_near[k].wait_recv()
        g_far[k].wait_recv()
        at = rows_at(h * QUART + k * PIECE, PIECE)
        back(1, k, gp[0, at] + gprecv[1, cut(k)].astype(F32) + gprecv[2, cut(k)].astype(F32))
    gather(gathered(1, 4), b // 8, 8, z_peer)
    settle(middle)
    for k in pieces:
        home_z[k].wait_recv()
        back(0, k, gr[piece(0, c, k)] + grrecv[4, cut(k)].astype(F32))
        if k == 0:
            product(1, slice(0, QUART))
        if k == 1:
            product(0, slice(0, 2 * PIECE))
            forward(1)
    product(0, slice(2 * PIECE, QUART))

    def place(w, half, block):
        @pl.when(half == 0)
        def _():
            oval[w, :, :HALF] = block

        @pl.when(half == 1)
        def _():
            oval[w, :, HALF:] = block

    for w in (1, 0):
        if w == 0:
            settle(links)
            forward(0)
        for link in o_near[w]:
            link.wait_recv()
        place(w, h, onear[w].astype(F32).T.astype(BF))
        for link in d_sib[w]:
            link.wait_recv()
        place(w, 1 - h, dot(projs[w, 0], dbuf[w], NT).astype(BF))
    loss_ref[0] = jnp.sum(gathered(2, 8)) / (ROWS * BLOCKS * STEPS * ROWS)
    settle(links)


def deliver(grads, out_r, out_p, sem):
    copies = [pltpu.make_async_copy(grads.at[w], (out_r, out_p)[w], sem.at[w]) for w in (0, 1)]
    for copy in copies:
        copy.start()
    for copy in copies:
        copy.wait()


def on_device(
    prompt_feats, response_feats, prompt_proj, response_proj,
    logit_scale, logit_bias, teacher, valid,
):
    anywhere = pl.BlockSpec(memory_space=pl.ANY)
    scalar = pl.BlockSpec(memory_space=pltpu.SMEM)

    def vm(*shape, kind=BF):
        return pltpu.VMEM(shape, kind)

    grads, loss = pl.pallas_call(
        kernel,
        out_shape=(
            pltpu.VMEM((2, FEAT, ROWS), BF),
            jax.ShapeDtypeStruct((1,), F32),
        ),
        in_specs=[anywhere] * 4 + [scalar] * 2 + [anywhere] * 2,
        out_specs=(pl.BlockSpec(memory_space=pltpu.VMEM), scalar),
        scratch_shapes=[
            vm(2, FEAT, ROWS),
            vm(2, ROWS, FEAT),
            vm(2, 2, FEAT, EMB),
            vm(2, HALF, EMB, kind=F32),
            vm(2, QUART, EMB),
            vm(2, QUART, EMB),
            vm(2, 2, QUART, FEAT),
            vm(2, QUART, EMB),
            vm(2, QUART, EMB),
            vm(2, QUART, EMB, kind=F32),
            vm(2, QUART, 128, kind=F32),
            vm(2, HALF, EMB),
            vm(SLOTS * HALF, EMB),
            vm(2, QUART, STEPS * ROWS, kind=jnp.int32),
            vm(2, HALF, ROWS),
            vm(2, HALF, ROWS),
            vm(2, 2, HALF, ROWS, kind=F32),
            vm(2, STEPS, ROWS, kind=jnp.int32),
            vm(2, ROWS, STEPS, kind=F32),
            vm(2, 2, HALF, ROWS),
            vm(2, HALF, EMB, kind=F32),
            vm(SLOTS * HALF, EMB, kind=F32),
            vm(3, QUART, EMB),
            vm(3, QUART, EMB),
            vm(SLOTS, QUART, EMB),
            vm(SLOTS, QUART, EMB),
            vm(SLOTS, QUART, EMB),
            vm(SLOTS, QUART, EMB),
            vm(2, QUART, EMB),
            vm(2, HALF, EMB),
            vm(2, 2, QUART, FEAT),
            vm(2, HALF, FEAT),
            vm(8, ROWS, kind=F32),
            vm(3, 8, 128, kind=F32),
            vm(3, 8, 8, 128, kind=F32),
            pltpu.SemaphoreType.DMA((128,)),
            pltpu.SemaphoreType.DMA((128,)),
            pltpu.SemaphoreType.DMA((16,)),
        ],
        compiler_params=pltpu.CompilerParams(
            collective_id=0, has_side_effects=True, vmem_limit_bytes=56 * 2**20
        ),
        name="band",
    )(
        response_feats.T, prompt_feats.T, response_proj, prompt_proj,
        logit_scale, logit_bias, teacher, valid.T,
    )
    grad_response, grad_prompt = pl.pallas_call(
        deliver,
        out_shape=(jax.ShapeDtypeStruct((FEAT, ROWS), BF),) * 2,
        in_specs=[pl.BlockSpec(memory_space=pltpu.VMEM)],
        out_specs=(anywhere, anywhere),
        scratch_shapes=[pltpu.SemaphoreType.DMA((2,))],
        name="deliver",
    )(pltpu.with_memory_space_constraint(grads, pltpu.VMEM))
    return grad_prompt.T, grad_response.T, loss


def solution(mesh):
    in_specs = (
        P("batch", "tower"), P("batch", "tower"), P("tower", None), P("tower", None),
        P(), P(), P("batch", None), P("batch", None),
    )
    out_specs = (P("batch", "tower"), P("batch", "tower"), P())
    return jax.shard_map(
        on_device, mesh=mesh, in_specs=in_specs, out_specs=out_specs, check_vma=False
    )
```
